256 devices in a mesh: dp: 32 (over z, y), tensor: 8 (over x, core).
Axes of the slice: x: 4, y: 4, z: 8, core: 2. Of those that a mesh axis runs over, the one named last changes fastest.
Arguments:
- hidden: bfloat16 [256, 5376], P('dp', 'tensor'), may hold values from -24 to 24
- tangent: bfloat16 [256, 5376], P('dp', 'tensor'), may hold values from -6 to 6
- out_weight: bfloat16 [262144, 5376], P(('dp', 'tensor')), may hold values from -2 to 2
Outputs:
- gn_product: float32 [256, 5376], P('dp', 'tensor')
The draws below stay inside these ranges and needn't reach their ends.
All inputs are finite; a program needn't handle non-finite values.
Results may differ from the reference program's by a relative error of at most 0.0045.
Values may be sent and summed in bfloat16 or wider, within the bound.
No kernel may reach another device: no remote copies, remote signals or barrier semaphores. Data moves between devices by JAX's collectives and lax.ppermute only.
A program may use at most 64 MiB of HBM per device.

```python
import math
import jax
import jax.numpy as jnp

D = 5376
TOKENS = 256
VOCAB = 262144


def aligned_rows(key):
    position = jnp.arange(D)
    first_half = (position < D // 2).astype(jnp.float32)
    sign_pattern = jnp.where(jax.random.bernoulli(jax.random.fold_in(key, 14), 0.5, (D,)), 1.0, -1.0).astype(jnp.float32)
    alternate = jnp.where(position % 2 == 0, 1.0, -1.0).astype(jnp.float32)
    common = sign_pattern * alternate * (1.0 - first_half) / math.sqrt(D // 2)
    return (sign_pattern, common)


def draw_out_weight(key, part):
    sign_pattern, common = aligned_rows(key)
    key = jax.random.fold_in(key, 1)
    jitter = jax.random.normal(jax.random.fold_in(key, 2), (VOCAB, D), jnp.float32)
    spread = 0.15 * jnp.exp(jax.random.uniform(jax.random.fold_in(key, 3), (VOCAB, 1), jnp.float32) * math.log(10.0))
    uniform_level = jax.random.uniform(jax.random.fold_in(key, 7), (VOCAB, 1), jnp.float32, 1e-06, 1.0)
    offset = jnp.minimum(-jnp.log(uniform_level), 12.0)
    loading = jnp.clip(jax.random.normal(jax.random.fold_in(key, 9), (VOCAB, 1), jnp.float32), -4.0, 4.0)
    matrix = spread * jnp.clip(jitter, -5.0, 5.0) / math.sqrt(D) - offset * sign_pattern[None, :] / D + 0.6 * loading * common[None, :]
    return matrix.astype(jnp.bfloat16)


def draw_hidden(key, part):
    sign_pattern, common = aligned_rows(key)
    key = jax.random.fold_in(key, 2)
    scales = jnp.exp(jax.random.uniform(jax.random.fold_in(key, 6), (TOKENS, 1), jnp.float32) * math.log(2.0))
    lift_draw = jax.random.uniform(jax.random.fold_in(key, 8), (TOKENS, 1), jnp.float32)
    jitter = jnp.clip(jax.random.normal(jax.random.fold_in(key, 5), (TOKENS, D), jnp.float32), -5.0, 5.0)
    lift_size = 2.5 + 1.5 * lift_draw
    values = scales * jitter + lift_size * sign_pattern[None, :]
    quiet_rows = (jnp.arange(TOKENS) % 8 == 7)[:, None]
    values = jnp.where(quiet_rows, 0.05 * jitter + 0.1 * sign_pattern[None, :], values)
    return values.astype(jnp.bfloat16)


def block_scale(stream_key, shape, shards, smallest, high):
    def one(dim, shards_of):
        heights = jax.random.uniform(jax.random.fold_in(jax.random.fold_in(stream_key, 6), dim), (shards_of,), jnp.float32, smallest / len(shards), high / len(shards))
        return jnp.repeat(jnp.exp(heights), shape[dim] // shards_of).reshape((-1,) + (1,) * (len(shape) - dim - 1))

    gain = one(*shards[0])
    for cut in shards[1:]:
        gain = gain * one(*cut)
    return gain


def noise(stream_key, dims, deviation, most, cuts=(), held_as=jnp.bfloat16):
    entries = deviation * jax.random.normal(stream_key, dims, jnp.float32)
    if cuts:
        entries = entries * block_scale(stream_key, dims, cuts, -0.22, 0.18)
    return jnp.clip(entries, -most, most).astype(held_as)


def setup_inputs(seed: int = 0) -> dict:
    splits = jax.random.split(jax.random.key(seed), 4)
    return {
        "hidden": draw_hidden(jax.random.fold_in(splits[3], 71), 0),
        "tangent": noise(splits[1], (TOKENS, D), 1.0, 6.0, ((0, 32), (1, 8))),
        "out_weight": draw_out_weight(jax.random.fold_in(splits[3], 71), 0),
    }


def reference(hidden, tangent, out_weight):
    scores = jnp.dot(hidden, out_weight.T, preferred_element_type=jnp.float32)
    slopes = jnp.dot(tangent, out_weight.T, preferred_element_type=jnp.float32)
    row_top = jnp.max(scores, axis=1, keepdims=True)
    weights_exp = jnp.exp(scores - row_top)
    totals = jnp.sum(weights_exp, axis=1, keepdims=True)
    dotted = jnp.sum(weights_exp * slopes, axis=1, keepdims=True)
    mixture = ((weights_exp / totals) * (slopes - dotted / totals)).astype(jnp.bfloat16)
    return jnp.dot(mixture, out_weight, preferred_element_type=jnp.float32)
```

```python
import functools

import jax
import jax.numpy as jnp
from jax import lax
from jax.experimental import pallas as pl
from jax.experimental.pallas import tpu as pltpu
from jax.sharding import Mesh, PartitionSpec as P

AXES = ("z", "y", "x", "c")
BF = jnp.bfloat16
F32 = jnp.float32
VMEM = pl.BlockSpec(memory_space=pltpu.VMEM)
ANY = pl.BlockSpec(memory_space=pl.ANY)
LIMIT = pltpu.CompilerParams(vmem_limit_bytes=56 * 1024 * 1024)
NZ, NQ = 8, 4


def perm(move):
    pairs = []
    for z in range(NZ):
        for y in range(NQ):
            for x in range(NQ):
                for c in range(2):
                    tz, ty, tx, tc = move(z, y, x, c)
                    src = ((z * NQ + y) * NQ + x) * 2 + c
                    dst = ((tz % NZ * NQ + ty % NQ) * NQ + tx % NQ) * 2 + tc
                    pairs.append((src, dst))
    return pairs


def send(value, move):
    return lax.ppermute(value, AXES, perm(move))


def along_z(k):
    return lambda z, y, x, c: (z + k, y, x, c)


def along_y(k):
    return lambda z, y, x, c: (z, y + k, x, c)


def along_x(k):
    return lambda z, y, x, c: (z, y, x + k, c)


def along_yx(k):
    return lambda z, y, x, c: (z, y + k, x, c) if c == 0 else (z, y, x + k, c)


def along_xy(k):
    return lambda z, y, x, c: (z, y, x + k, c) if c == 0 else (z, y + k, x, c)


def other_core(z, y, x, c):
    return (z, y, x, 1 - c)


HOPS = (1, 3, 2)
ZHOPS = (4, 3, 5, 2, 6, 1, 7)


def place_z(*refs):
    *pieces, out, held = refs
    z = lax.axis_index("z")
    for k, piece in enumerate(pieces):
        both = piece[...].astype(F32)
        at = lax.rem(z + (NZ - k), NZ)
        held[0, at] = both[:8]
        held[1, at] = both[8:]
    out[...] = held[...].reshape(out.shape).astype(BF)


def scores_kernel(*refs):
    pieces = refs[: 2 * NQ]
    w, scores, slopes, stats, held, whole, sems = refs[2 * NQ :]
    step = pl.program_id(0)
    rows = w.shape[0]
    tokens = scores.shape[1]
    width = held.shape[-1]

    @pl.when(step == 0)
    def _():
        y, x, c = lax.axis_index("y"), lax.axis_index("x"), lax.axis_index("c")
        copies = []
        for own in range(2):
            parity = c if own == 0 else 1 - c
            for k in range(NQ):
                for r in range(NQ):
                    x_back = jnp.where(parity == 0, k, r)
                    y_back = jnp.where(parity == 0, r, k)
                    x_at = lax.rem(x + NQ - x_back, NQ)
                    y_at = lax.rem(y + NQ - y_back, NQ)
                    copy = pltpu.make_async_copy(
                        pieces[own * NQ + k].at[r],
                        held.at[2 * x_at + parity, :, y_at],
                        sems.at[own, k, r],
                    )
                    copy.start()
                    copies.append(copy)
        for copy in copies:
            copy.wait()
        for t in range(2 * NQ):
            whole[:, t * width : (t + 1) * width] = held[t].reshape(2 * tokens, width)

    at = pl.ds(pl.multiple_of(step * rows, rows), rows)
    both = lax.dot_general(
        w[...], whole[...], (((1,), (1,)), ((), ())), preferred_element_type=F32
    )
    scores[at, :] = both[:, :tokens]
    slopes[at, :] = both[:, tokens:]

    @pl.when(step == pl.num_programs(0) - 1)
    def _():
        top = jnp.max(scores[...], axis=0, keepdims=True)
        raised = jnp.exp(scores[...] - top)
        scores[...] = raised
        stats[0:1, :] = top
        stats[1:2, :] = jnp.sum(raised, axis=0, keepdims=True)
        stats[2:3, :] = jnp.sum(raised * slopes[...], axis=0, keepdims=True)
        stats[3:8, :] = jnp.zeros((5, tokens), F32)


def merged(refs):
    top = refs[0][0:1, :]
    for ref in refs[1:]:
        top = jnp.maximum(top, ref[0:1, :])
    total = dotted = 0.0
    for ref in refs:
        scale = jnp.exp(ref[0:1, :] - top)
        total = total + scale * ref[1:2, :]
        dotted = dotted + scale * ref[2:3, :]
    return top, total, dotted


def merge_kernel(*refs):
    *parts, out = refs
    out[0:1, :], out[1:2, :], out[2:3, :] = merged(parts)
    out[3:8, :] = jnp.zeros((5, out.shape[1]), F32)


def product_kernel(*refs):
    parts = refs[:NZ]
    mine, raised, slopes, w, keep, give, mixture = refs[NZ:]
    step = pl.program_id(0)
    tokens = mixture.shape[0]
    width = keep.shape[-1]
    part = tokens // NQ

    @pl.when(step == 0)
    def _():
        top, total, dotted = merged(parts)
        scale = jnp.exp(mine[0:1, :] - top) / total
        mean = dotted / total
        mix = (raised[...] * scale) * (slopes[...] - mean)
        mixture[...] = mix.T.astype(BF)

    y, x, c = lax.axis_index("y"), lax.axis_index("x"), lax.axis_index("c")
    product = jnp.dot(mixture[...], w[...], preferred_element_type=F32)
    for half in range(2):
        x_of = 2 * step + half
        x_ahead = lax.rem(x_of + NQ - x, NQ)
        for parity in range(2):
            at = (2 * half + parity) * width
            piece = product[:, at : at + width]
            for y_of in range(NQ):
                rows = piece[y_of * part : (y_of + 1) * part]
                y_ahead = lax.rem(y_of + NQ - y, NQ)
                k, r = (x_ahead, y_ahead) if parity == 0 else (y_ahead, x_ahead)

                @pl.when(c == parity)
                def _():
                    keep[k, r] = rows

                @pl.when(c != parity)
                def _():
                    give[k, r] = rows.astype(BF)


def sum_to_z(own, *refs):
    *parts, out0, out1, out2, out3, out4, out5, out6, out7, held = refs
    total = own[...]
    for part in parts:
        total = total + part[...].astype(F32)
    held[...] = total.reshape(held.shape)
    z = lax.axis_index("z")
    for k, out in enumerate((out0, out1, out2, out3, out4, out5, out6, out7)):
        out[...] = held[lax.rem(z + k, NZ)]


def per_device(hidden, tangent, out_weight):
    rows, width = hidden.shape
    vocab, features = out_weight.shape
    tokens = rows * NZ * NQ
    shape = jax.ShapeDtypeStruct

    with jax.named_scope("gather_z"):
        own = jnp.concatenate((hidden, tangent), 0)
        pieces = {0: own}
        for k in ZHOPS:
            pieces[k] = send(own, along_z(k))
        block = pl.pallas_call(
            place_z,
            out_shape=shape((2, rows * NZ, width), BF),
            in_specs=[VMEM] * NZ,
            out_specs=VMEM,
            scratch_shapes=[pltpu.VMEM((2, NZ, rows, width), F32)],
            compiler_params=LIMIT,
        )(*(pieces[k] for k in range(NZ)))
    with jax.named_scope("gather_yx"):
        pieces = {0: block}
        for k in HOPS:
            pieces[k] = send(block, along_yx(k))
        block = jnp.stack([pieces[k] for k in range(NQ)])
    with jax.named_scope("gather_xy"):
        pieces = {0: block}
        for k in HOPS:
            pieces[k] = send(block, along_xy(k))
        theirs = {k: send(pieces[k], other_core) for k in (0,) + HOPS}

    steps = 4
    with jax.named_scope("scores"):
        raised, slopes, mine = pl.pallas_call(
            scores_kernel,
            grid=(steps,),
            out_shape=(
                shape((vocab, tokens), F32),
                shape((vocab, tokens), F32),
                shape((8, tokens), F32),
            ),
            in_specs=[ANY] * (2 * NQ)
            + [pl.BlockSpec((vocab // steps, features), lambda i: (i, 0))],
            out_specs=(
                pl.BlockSpec((vocab, tokens), lambda i: (0, 0)),
                pl.BlockSpec((vocab, tokens), lambda i: (0, 0)),
                pl.BlockSpec((8, tokens), lambda i: (0, 0)),
            ),
            scratch_shapes=[
                pltpu.VMEM((2 * NQ, 2, NQ, rows * NZ, width), BF),
                pltpu.VMEM((2 * tokens, features), BF),
                pltpu.SemaphoreType.DMA((2, NQ, NQ)),
            ],
            compiler_params=LIMIT,
        )(*(pieces[k] for k in range(NQ)), *(theirs[k] for k in range(NQ)), out_weight)

    with jax.named_scope("statistics"):
        stats = mine
        for move, hops in ((None, (1,)), (along_x, HOPS), (along_y, HOPS)):
            parts = [stats] + [send(stats, move(k) if move else other_core) for k in hops]
            stats = pl.pallas_call(
                merge_kernel,
                out_shape=shape((8, tokens), F32),
                in_specs=[VMEM] * len(parts),
                out_specs=VMEM,
            )(*parts)
        parts = [stats] + [send(stats, along_z(k)) for k in ZHOPS]

    with jax.named_scope("product"):
        whole = lambda n: pl.BlockSpec(n, lambda i: (0,) * len(n))
        keep, give = pl.pallas_call(
            product_kernel,
            grid=(2,),
            out_shape=(
                shape((NQ, NQ, rows * NZ, width), F32),
                shape((NQ, NQ, rows * NZ, width), BF),
            ),
            in_specs=[whole((8, tokens))] * (NZ + 1)
            + [whole((vocab, tokens))] * 2
            + [pl.BlockSpec((vocab, features // 2), lambda i: (0, i))],
            out_specs=(
                whole((NQ, NQ, rows * NZ, width)),
                whole((NQ, NQ, rows * NZ, width)),
            ),
            scratch_shapes=[pltpu.VMEM((tokens, vocab), BF)],
            compiler_params=LIMIT,
        )(*parts, mine, raised, slopes, out_weight)

    with jax.named_scope("scatter_core"):
        got = send(give, other_core)
    with jax.named_scope("scatter_xy"):
        sums = [keep[k] + got[k].astype(F32) for k in range(NQ)]
        total = sums[0]
        for k in HOPS:
            total = total + send(sums[k].astype(BF), along_xy(k)).astype(F32)
    with jax.named_scope("scatter_yx"):
        parts = [send(total[k].astype(BF), along_yx(k)) for k in HOPS]
        outs = pl.pallas_call(
            sum_to_z,
            out_shape=[shape((rows, width), F32)] * NZ,
            in_specs=[VMEM] * (1 + len(parts)),
            out_specs=[VMEM] * NZ,
            scratch_shapes=[pltpu.VMEM((NZ, rows, width), F32)],
            compiler_params=LIMIT,
        )(total[0], *parts)
    with jax.named_scope("scatter_z"):
        result = outs[0]
        for k in ZHOPS:
            result = result + send(outs[k], along_z(k))
    return result


def solution(mesh):
    fine = Mesh(mesh.devices.reshape(NZ, NQ, NQ, 2), AXES)
    tokens = P(("z", "y"), ("x", "c"))
    return jax.shard_map(
        per_device,
        mesh=fine,
        in_specs=(tokens, tokens, P(AXES, None)),
        out_specs=tokens,
        check_vma=False,
    )
```

```python
import functools

import jax
import jax.numpy as jnp
from jax import lax
from jax.experimental import pallas as pl
from jax.experimental.pallas import tpu as pltpu
from jax.sharding import Mesh, PartitionSpec as P

AXES = ("z", "y", "x", "c")
BF = jnp.bfloat16
F32 = jnp.float32
VMEM = pl.BlockSpec(memory_space=pltpu.VMEM)
ANY = pl.BlockSpec(memory_space=pl.ANY)
MIB = 1024 * 1024
NZ, NQ = 8, 4


def perm(move):
    pairs = []
    for z in range(NZ):
        for y in range(NQ):
            for x in range(NQ):
                for c in range(2):
                    tz, ty, tx, tc = move(z, y, x, c)
                    src = ((z * NQ + y) * NQ + x) * 2 + c
                    dst = ((tz % NZ * NQ + ty % NQ) * NQ + tx % NQ) * 2 + tc
                    pairs.append((src, dst))
    return pairs


def send(value, move):
    return lax.ppermute(value, AXES, perm(move))


def along_yx(k):
    return lambda z, y, x, c: (z, y + k, x, c) if c == 0 else (z, y, x + k, c)


def along_xy(k):
    return lambda z, y, x, c: (z, y, x + k, c) if c == 0 else (z, y + k, x, c)


def other_core(z, y, x, c):
    return (z, y, x, 1 - c)


HOPS = (1, 3, 2)


def all_of(value, axes):
    return lax.all_to_all(value, axes, 0, 0)


def scores_kernel(*refs):
    pieces = refs[: 2 * NQ]
    w, scores, slopes, stats, held, whole, sems = refs[2 * NQ :]
    step = pl.program_id(0)
    rows = w.shape[0]
    tokens = scores.shape[1]
    width = held.shape[-1]

    @pl.when(step == 0)
    def _():
        y, x, c = lax.axis_index("y"), lax.axis_index("x"), lax.axis_index("c")
        copies = []
        for own in range(2):
            parity = c if own == 0 else 1 - c
            for k in range(NQ):
                for r in range(NQ):
                    x_back = jnp.where(parity == 0, k, r)
                    y_back = jnp.where(parity == 0, r, k)
                    x_at = lax.rem(x + NQ - x_back, NQ)
                    y_at = lax.rem(y + NQ - y_back, NQ)
                    copy = pltpu.make_async_copy(
                        pieces[own * NQ + k].at[r],
                        held.at[2 * x_at + parity, :, y_at],
                        sems.at[own, k, r],
                    )
                    copy.start()
                    copies.append(copy)
        for copy in copies:
            copy.wait()
        for t in range(2 * NQ):
            whole[:, t * width : (t + 1) * width] = held[t].reshape(2 * tokens, width)

    at = pl.ds(pl.multiple_of(step * rows, rows), rows)
    both = lax.dot_general(
        w[...], whole[...], (((1,), (1,)), ((), ())), preferred_element_type=F32
    )
    scores[at, :] = both[:, :tokens]
    slopes[at, :] = both[:, tokens:]

    @pl.when(step == pl.num_programs(0) - 1)
    def _():
        top = jnp.max(scores[...], axis=0, keepdims=True)
        raised = jnp.exp(scores[...] - top)
        scores[...] = raised
        own = jnp.concatenate(
            (
                top,
                jnp.sum(raised, axis=0, keepdims=True),
                jnp.sum(raised * slopes[...], axis=0, keepdims=True),
                jnp.zeros((5, tokens), F32),
            ),
            0,
        )
        stats[...] = jnp.broadcast_to(own[None], stats.shape)


def merged(parts):
    tops = parts[:, 0]
    top = jnp.max(tops, axis=0, keepdims=True)
    scale = jnp.exp(tops - top)
    total = jnp.sum(scale * parts[:, 1], axis=0, keepdims=True)
    dotted = jnp.sum(scale * parts[:, 2], axis=0, keepdims=True)
    return top, total, dotted


def merge_kernel(parts, out):
    rest = jnp.zeros((5, out.shape[-1]), F32)
    own = jnp.concatenate((*merged(parts[...]), rest), 0)
    out[...] = jnp.broadcast_to(own[None], out.shape)


def product_kernel(parts, mine, raised, slopes, w, keep, give, mixture):
    step = pl.program_id(0)
    tokens = mixture.shape[0]
    width = keep.shape[-1]
    part = tokens // NQ

    @pl.when(step == 0)
    def _():
        top, total, dotted = merged(parts[...])
        scale = jnp.exp(mine[0, 0:1, :] - top) / total
        mean = dotted / total
        mix = (raised[...] * scale) * (slopes[...] - mean)
        mixture[...] = mix.T.astype(BF)

    y, x, c = lax.axis_index("y"), lax.axis_index("x"), lax.axis_index("c")
    product = jnp.dot(mixture[...], w[...], preferred_element_type=F32)
    for half in range(2):
        x_of = 2 * step + half
        x_ahead = lax.rem(x_of + NQ - x, NQ)
        for parity in range(2):
            at = (2 * half + parity) * width
            piece = product[:, at : at + width]
            for y_of in range(NQ):
                rows = piece[y_of * part : (y_of + 1) * part]
                y_ahead = lax.rem(y_of + NQ - y, NQ)
                k, r = (x_ahead, y_ahead) if parity == 0 else (y_ahead, x_ahead)

                @pl.when(c == parity)
                def _():
                    keep[k, r] = rows

                @pl.when(c != parity)
                def _():
                    give[k, r] = rows.astype(BF)


def per_device(hidden, tangent, out_weight):
    rows, width = hidden.shape
    vocab, features = out_weight.shape
    tokens = rows * NZ * NQ
    shape = jax.ShapeDtypeStruct

    with jax.named_scope("gather_z"):
        own = jnp.stack((hidden, tangent))
        block = all_of(jnp.broadcast_to(own[None], (NZ, *own.shape)), "z")
        block = block.transpose(1, 0, 2, 3).reshape(2, rows * NZ, width)
    with jax.named_scope("gather_yx"):
        pieces = {0: block}
        for k in HOPS:
            pieces[k] = send(block, along_yx(k))
        block = jnp.stack([pieces[k] for k in range(NQ)])
    with jax.named_scope("gather_xy"):
        pieces = {0: block}
        for k in HOPS:
            pieces[k] = send(block, along_xy(k))
        theirs = {k: send(pieces[k], other_core) for k in (0,) + HOPS}

    steps = 4
    with jax.named_scope("scores"):
        raised, slopes, mine = pl.pallas_call(
            scores_kernel,
            grid=(steps,),
            out_shape=(
                shape((vocab, tokens), F32),
                shape((vocab, tokens), F32),
                shape((2 * NQ, 8, tokens), F32),
            ),
            in_specs=[ANY] * (2 * NQ)
            + [pl.BlockSpec((vocab // steps, features), lambda i: (i, 0))],
            out_specs=(
                pl.BlockSpec((vocab, tokens), lambda i: (0, 0)),
                pl.BlockSpec((vocab, tokens), lambda i: (0, 0)),
                pl.BlockSpec((2 * NQ, 8, tokens), lambda i: (0, 0, 0)),
            ),
            scratch_shapes=[
                pltpu.VMEM((2 * NQ, 2, NQ, rows * NZ, width), BF),
                pltpu.VMEM((2 * tokens, features), BF),
                pltpu.SemaphoreType.DMA((2, NQ, NQ)),
            ],
            compiler_params=pltpu.CompilerParams(vmem_limit_bytes=32 * MIB),
        )(*(pieces[k] for k in range(NQ)), *(theirs[k] for k in range(NQ)), out_weight)

    with jax.named_scope("statistics"):
        stats = pl.pallas_call(
            merge_kernel,
            out_shape=shape((NZ * NQ, 8, tokens), F32),
            in_specs=[VMEM],
            out_specs=VMEM,
        )(all_of(mine, ("x", "c")))
        parts = all_of(stats, ("z", "y"))

    with jax.named_scope("product"):
        whole = lambda n: pl.BlockSpec(n, lambda i: (0,) * len(n))
        keep, give = pl.pallas_call(
            product_kernel,
            grid=(2,),
            out_shape=(
                shape((NQ, NQ, rows * NZ, width), F32),
                shape((NQ, NQ, rows * NZ, width), BF),
            ),
            in_specs=[whole((NZ * NQ, 8, tokens)), whole((1, 8, tokens))]
            + [whole((vocab, tokens))] * 2
            + [pl.BlockSpec((vocab, features // 2), lambda i: (0, i))],
            out_specs=(
                whole((NQ, NQ, rows * NZ, width)),
                whole((NQ, NQ, rows * NZ, width)),
            ),
            scratch_shapes=[pltpu.VMEM((tokens, vocab), BF)],
            compiler_params=pltpu.CompilerParams(vmem_limit_bytes=40 * MIB),
        )(parts, mine, raised, slopes, out_weight)

    with jax.named_scope("scatter_core"):
        got = send(give, other_core)
    with jax.named_scope("scatter_xy"):
        sums = [keep[k] + got[k].astype(F32) for k in range(NQ)]
        total = sums[0]
        for k in HOPS:
            total = total + send(sums[k].astype(BF), along_xy(k)).astype(F32)
    with jax.named_scope("scatter_yx"):
        total, rest = total[0], total
        for k in HOPS:
            total = total + send(rest[k].astype(BF), along_yx(k)).astype(F32)
    with jax.named_scope("scatter_z"):
        return jnp.sum(all_of(total.reshape(NZ, rows, width), "z"), axis=0)


def solution(mesh):
    fine = Mesh(mesh.devices.reshape(NZ, NQ, NQ, 2), AXES)
    tokens = P(("z", "y"), ("x", "c"))
    return jax.shard_map(
        per_device,
        mesh=fine,
        in_specs=(tokens, tokens, P(AXES, None)),
        out_specs=tokens,
        check_vma=False,
    )
```

```python
import functools

import jax
import jax.numpy as jnp
from jax import lax
from jax.experimental import pallas as pl
from jax.experimental.pallas import tpu as pltpu
from jax.sharding import Mesh, PartitionSpec as P

AXES = ("z", "y", "x", "c")
BF = jnp.bfloat16
F32 = jnp.float32
VMEM = pl.BlockSpec(memory_space=pltpu.VMEM)
ANY = pl.BlockSpec(memory_space=pl.ANY)
MIB = 1024 * 1024
NZ, NQ = 8, 4


def perm(move):
    pairs = []
    for z in range(NZ):
        for y in range(NQ):
            for x in range(NQ):
                for c in range(2):
                    tz, ty, tx, tc = move(z, y, x, c)
                    src = ((z * NQ + y) * NQ + x) * 2 + c
                    dst = ((tz % NZ * NQ + ty % NQ) * NQ + tx % NQ) * 2 + tc
                    pairs.append((src, dst))
    return pairs


def send(value, move):
    return lax.ppermute(value, AXES, perm(move))


def along_yx(k):
    return lambda z, y, x, c: (z, y + k, x, c) if c == 0 else (z, y, x + k, c)


def along_xy(k):
    return lambda z, y, x, c: (z, y, x + k, c) if c == 0 else (z, y + k, x, c)


def other_core(z, y, x, c):
    return (z, y, x, 1 - c)


HOPS = (1, 3, 2)


def all_of(value, axes):
    return lax.all_to_all(value, axes, 0, 0)


def load_kernel(w, _, out, sem):
    copy = pltpu.make_async_copy(w, out, sem)
    copy.start()
    copy.wait()


def scores_kernel(*refs):
    pieces = refs[: 2 * NQ]
    w, scores, slopes, stats, held, whole = refs[2 * NQ :]
    step = pl.program_id(0)
    rows = w.shape[0] // pl.num_programs(0)
    tokens = scores.shape[1]
    width = held.shape[-1]

    @pl.when(step == 0)
    def _():
        y, x, c = lax.axis_index("y"), lax.axis_index("x"), lax.axis_index("c")
        for own in range(2):
            parity = c if own == 0 else 1 - c
            for k in range(NQ):
                for r in range(NQ):
                    x_back = jnp.where(parity == 0, k, r)
                    y_back = jnp.where(parity == 0, r, k)
                    x_at = lax.rem(x + NQ - x_back, NQ)
                    y_at = lax.rem(y + NQ - y_back, NQ)
                    for half in range(2):
                        held[2 * x_at + parity, half, y_at] = pieces[own * NQ + k][r, half]
        for t in range(2 * NQ):
            whole[:, t * width : (t + 1) * width] = held[t].reshape(2 * tokens, width)

    at = pl.ds(pl.multiple_of(step * rows, rows), rows)
    both = lax.dot_general(
        w[at, :], whole[...], (((1,), (1,)), ((), ())), preferred_element_type=F32
    )
    scores[at, :] = both[:, :tokens]
    slopes[at, :] = both[:, tokens:]

    @pl.when(step == pl.num_programs(0) - 1)
    def _():
        top = jnp.max(scores[...], axis=0, keepdims=True)
        raised = jnp.exp(scores[...] - top)
        scores[...] = raised
        own = jnp.concatenate(
            (
                top,
                jnp.sum(raised, axis=0, keepdims=True),
                jnp.sum(raised * slopes[...], axis=0, keepdims=True),
                jnp.zeros((5, tokens), F32),
            ),
            0,
        )
        stats[...] = jnp.broadcast_to(own[None], stats.shape)


def merged(parts):
    tops = parts[:, 0]
    top = jnp.max(tops, axis=0, keepdims=True)
    scale = jnp.exp(tops - top)
    total = jnp.sum(scale * parts[:, 1], axis=0, keepdims=True)
    dotted = jnp.sum(scale * parts[:, 2], axis=0, keepdims=True)
    return top, total, dotted


def merge_kernel(parts, out):
    rest = jnp.zeros((5, out.shape[-1]), F32)
    own = jnp.concatenate((*merged(parts[...]), rest), 0)
    out[...] = jnp.broadcast_to(own[None], out.shape)


def product_kernel(parts, mine, raised, slopes, w, keep, give, mixture):
    tokens = mixture.shape[0]
    width = keep.shape[-1]
    part = tokens // NQ

    top, total, dotted = merged(parts[...])
    scale = jnp.exp(mine[0, 0:1, :] - top) / total
    mean = dotted / total
    mix = (raised[...] * scale) * (slopes[...] - mean)
    mixture[...] = mix.T.astype(BF)

    y, x, c = lax.axis_index("y"), lax.axis_index("x"), lax.axis_index("c")
    for pair in range(2):
        columns = slice(pair * 4 * width, (pair + 1) * 4 * width)
        product = jnp.dot(mixture[...], w[:, columns], preferred_element_type=F32)
        for half in range(2):
            x_of = 2 * pair + half
            x_ahead = lax.rem(x_of + NQ - x, NQ)
            for parity in range(2):
                at = (2 * half + parity) * width
                piece = product[:, at : at + width]
                for y_of in range(NQ):
                    rows = piece[y_of * part : (y_of + 1) * part]
                    y_ahead = lax.rem(y_of + NQ - y, NQ)
                    k, r = (x_ahead, y_ahead) if parity == 0 else (y_ahead, x_ahead)

                    @pl.when(c == parity)
                    def _():
                        keep[k, r] = rows

                    @pl.when(c != parity)
                    def _():
                        give[k, r] = rows.astype(BF)


def per_device(hidden, tangent, out_weight):
    rows, width = hidden.shape
    vocab, features = out_weight.shape
    tokens = rows * NZ * NQ
    shape = jax.ShapeDtypeStruct

    with jax.named_scope("gather_z"):
        own = jnp.stack((hidden, tangent))
        block = all_of(jnp.broadcast_to(own[None], (NZ, *own.shape)), "z")
        block = block.transpose(1, 0, 2, 3).reshape(2, rows * NZ, width)
    with jax.named_scope("gather_yx"):
        pieces = {0: block}
        for k in HOPS:
            pieces[k] = send(block, along_yx(k))
        block = jnp.stack([pieces[k] for k in range(NQ)])
        weight = pl.pallas_call(
            load_kernel,
            out_shape=pltpu.VMEM((vocab, features), BF),
            in_specs=[ANY, ANY],
            out_specs=VMEM,
            scratch_shapes=[pltpu.SemaphoreType.DMA],
            cost_estimate=pl.CostEstimate(
                flops=0, transcendentals=0, bytes_accessed=4 * vocab * features
            ),
            compiler_params=pltpu.CompilerParams(vmem_limit_bytes=MIB),
        )(pltpu.with_memory_space_constraint(out_weight, pltpu.HBM), block)
    with jax.named_scope("gather_xy"):
        pieces = {0: block}
        for k in HOPS:
            pieces[k] = send(block, along_xy(k))
        pieces[HOPS[0]], weight = lax.optimization_barrier((pieces[HOPS[0]], weight))
        theirs = {k: send(pieces[k], other_core) for k in (0,) + HOPS}

    steps = 4
    with jax.named_scope("scores"):
        raised, slopes, mine = pl.pallas_call(
            scores_kernel,
            grid=(steps,),
            out_shape=(
                shape((vocab, tokens), F32),
                shape((vocab, tokens), F32),
                shape((2 * NQ, 8, tokens), F32),
            ),
            in_specs=[VMEM] * (2 * NQ + 1),
            out_specs=(
                pl.BlockSpec((vocab, tokens), lambda i: (0, 0)),
                pl.BlockSpec((vocab, tokens), lambda i: (0, 0)),
                pl.BlockSpec((2 * NQ, 8, tokens), lambda i: (0, 0, 0)),
            ),
            scratch_shapes=[
                pltpu.VMEM((2 * NQ, 2, NQ, rows * NZ, width), BF),
                pltpu.VMEM((2 * tokens, features), BF),
            ],
            compiler_params=pltpu.CompilerParams(vmem_limit_bytes=32 * MIB),
        )(*(pieces[k] for k in range(NQ)), *(theirs[k] for k in range(NQ)), weight)

    with jax.named_scope("statistics"):
        stats = pl.pallas_call(
            merge_kernel,
            out_shape=shape((NZ * NQ, 8, tokens), F32),
            in_specs=[VMEM],
            out_specs=VMEM,
            compiler_params=pltpu.CompilerParams(vmem_limit_bytes=4 * MIB),
        )(all_of(mine, ("x", "c")))
        parts = all_of(stats, ("z", "y"))

    with jax.named_scope("product"):
        keep, give = pl.pallas_call(
            product_kernel,
            out_shape=(
                shape((NQ, NQ, rows * NZ, width), F32),
                shape((NQ, NQ, rows * NZ, width), BF),
            ),
            in_specs=[VMEM] * 5,
            out_specs=(VMEM, VMEM),
            scratch_shapes=[pltpu.VMEM((tokens, vocab), BF)],
            compiler_params=pltpu.CompilerParams(vmem_limit_bytes=24 * MIB),
        )(parts, mine, raised, slopes, weight)

    with jax.named_scope("scatter_core"):
        got = send(give, other_core)
    with jax.named_scope("scatter_xy"):
        sums = [keep[k] + got[k].astype(F32) for k in range(NQ)]
        total = sums[0]
        for k in HOPS:
            total = total + send(sums[k].astype(BF), along_xy(k)).astype(F32)
    with jax.named_scope("scatter_yx"):
        total, rest = total[0], total
        for k in HOPS:
            total = total + send(rest[k].astype(BF), along_yx(k)).astype(F32)
    with jax.named_scope("scatter_z"):
        total = total.astype(BF).reshape(NZ, rows, width)
        return jnp.sum(all_of(total, "z").astype(F32), axis=0)


def solution(mesh):
    fine = Mesh(mesh.devices.reshape(NZ, NQ, NQ, 2), AXES)
    tokens = P(("z", "y"), ("x", "c"))
    return jax.shard_map(
        per_device,
        mesh=fine,
        in_specs=(tokens, tokens, P(AXES, None)),
        out_specs=tokens,
        check_vma=False,
    )
```

```python
import functools

import jax
import jax.numpy as jnp
from jax import lax
from jax.experimental import pallas as pl
from jax.experimental.pallas import tpu as pltpu
from jax.sharding import Mesh, PartitionSpec as P

AXES = ("z", "y", "x", "c")
BF = jnp.bfloat16
F32 = jnp.float32
VMEM = pl.BlockSpec(memory_space=pltpu.VMEM)
ANY = pl.BlockSpec(memory_space=pl.ANY)
MIB = 1024 * 1024
NZ, NQ = 8, 4


def perm(move):
    pairs = []
    for z in range(NZ):
        for y in range(NQ):
            for x in range(NQ):
                for c in range(2):
                    tz, ty, tx, tc = move(z, y, x, c)
                    src = ((z * NQ + y) * NQ + x) * 2 + c
                    dst = ((tz % NZ * NQ + ty % NQ) * NQ + tx % NQ) * 2 + tc
                    pairs.append((src, dst))
    return pairs


def send(value, move):
    return lax.ppermute(value, AXES, perm(move))


def along_yx(k):
    return lambda z, y, x, c: (z, y + k, x, c) if c == 0 else (z, y, x + k, c)


def along_xy(k):
    return lambda z, y, x, c: (z, y, x + k, c) if c == 0 else (z, y + k, x, c)


def other_core(z, y, x, c):
    return (z, y, x, 1 - c)


HOPS = (1, 3, 2)


def all_of(value, axes):
    return lax.all_to_all(value, axes, 0, 0)


def load_kernel(w, _, out, sem):
    copy = pltpu.make_async_copy(w, out, sem)
    copy.start()
    copy.wait()


def times_weight(refs, out):
    pieces = refs[: 2 * NQ]
    w, held, whole = refs[2 * NQ :]
    step = pl.program_id(0)
    rows = w.shape[0] // pl.num_programs(0)
    tokens, width = out.shape[1], held.shape[-1]

    @pl.when(step == 0)
    def _():
        y, x, c = lax.axis_index("y"), lax.axis_index("x"), lax.axis_index("c")
        for own in range(2):
            parity = c if own == 0 else 1 - c
            for k in range(NQ):
                for r in range(NQ):
                    x_back = jnp.where(parity == 0, k, r)
                    y_back = jnp.where(parity == 0, r, k)
                    x_at = lax.rem(x + NQ - x_back, NQ)
                    y_at = lax.rem(y + NQ - y_back, NQ)
                    held[2 * x_at + parity, y_at] = pieces[own * NQ + k][r]
        for t in range(2 * NQ):
            whole[:, t * width : (t + 1) * width] = held[t].reshape(tokens, width)

    at = pl.ds(pl.multiple_of(step * rows, rows), rows)
    out[at, :] = lax.dot_general(
        w[at, :], whole[...], (((1,), (1,)), ((), ())), preferred_element_type=F32
    )


def scores_kernel(*refs):
    raised, stats = refs[-4:-2]
    times_weight((*refs[:-4], *refs[-2:]), raised)

    @pl.when(pl.program_id(0) == pl.num_programs(0) - 1)
    def _():
        top = jnp.max(raised[...], axis=0, keepdims=True)
        value = jnp.exp(raised[...] - top)
        raised[...] = value
        total = jnp.sum(value, axis=0, keepdims=True)
        stats[...] = jnp.concatenate((top, total, total, total), 0)


def slopes_kernel(raised, top, *refs):
    slopes, stats = refs[-4:-2]
    times_weight((*refs[:-4], *refs[-2:]), slopes)

    @pl.when(pl.program_id(0) == pl.num_programs(0) - 1)
    def _():
        dotted = jnp.sum(raised[...] * slopes[...], axis=0, keepdims=True)
        own = jnp.concatenate((top[0:2, :], dotted, dotted), 0)
        stats[...] = jnp.broadcast_to(own[None], stats.shape)


def merged(parts):
    tops = parts[:, 0]
    top = jnp.max(tops, axis=0, keepdims=True)
    scale = jnp.exp(tops - top)
    total = jnp.sum(scale * parts[:, 1], axis=0, keepdims=True)
    dotted = jnp.sum(scale * parts[:, 2], axis=0, keepdims=True)
    return top, total, dotted


def merge_kernel(parts, out):
    top, total, dotted = merged(parts[...])
    own = jnp.concatenate((top, total, dotted, dotted), 0)
    out[...] = jnp.broadcast_to(own[None], out.shape)


def part_product(mixture, w, parity, out):
    y, x = lax.axis_index("y"), lax.axis_index("x")
    width, part = out.shape[-1], out.shape[-2]
    for x_of in range(NQ):
        first = (2 * x_of + parity) * width
        start = first // 128 * 128
        stop = -(-(first + width) // 128) * 128
        product = jnp.dot(mixture[...], w[:, start:stop], preferred_element_type=F32)
        piece = product[:, first - start : first - start + width].astype(out.dtype)
        x_ahead = lax.rem(x_of + NQ - x, NQ)
        for y_of in range(NQ):
            y_ahead = lax.rem(y_of + NQ - y, NQ)
            k, r = (x_ahead, y_ahead) if parity == 0 else (y_ahead, x_ahead)
            out[k, r] = piece[y_of * part : (y_of + 1) * part]


def give_kernel(parts, own_top, raised, slopes, w, give, mixture):
    top, total, dotted = merged(parts[...])
    scale = jnp.exp(own_top[0:1, :] - top) / total
    mean = dotted / total
    mix = (raised[...] * scale) * (slopes[...] - mean)
    mixture[...] = mix.T.astype(BF)
    for parity in range(2):
        pl.when(lax.axis_index("c") != parity)(
            functools.partial(part_product, mixture, w, parity, give)
        )


def keep_kernel(mixture, w, keep):
    for parity in range(2):
        pl.when(lax.axis_index("c") == parity)(
            functools.partial(part_product, mixture, w, parity, keep)
        )


def per_device(hidden, tangent, out_weight):
    rows, width = hidden.shape
    vocab, features = out_weight.shape
    tokens = rows * NZ * NQ
    shape = jax.ShapeDtypeStruct

    with jax.named_scope("gather_z"):
        own = jnp.stack((hidden, tangent))
        block = all_of(jnp.broadcast_to(own[None], (NZ, *own.shape)), "z")
        block = block.transpose(1, 0, 2, 3).reshape(2, rows * NZ, width)
    with jax.named_scope("gather_yx"):
        pieces = {0: block}
        for k in HOPS:
            pieces[k] = send(block, along_yx(k))
        blocks = [jnp.stack([pieces[k][i] for k in range(NQ)]) for i in range(2)]
        weight = pl.pallas_call(
            load_kernel,
            out_shape=pltpu.VMEM((vocab, features), BF),
            in_specs=[ANY, ANY],
            out_specs=VMEM,
            scratch_shapes=[pltpu.SemaphoreType.DMA],
            cost_estimate=pl.CostEstimate(
                flops=0, transcendentals=0, bytes_accessed=4 * vocab * features
            ),
            compiler_params=pltpu.CompilerParams(vmem_limit_bytes=MIB),
        )(pltpu.with_memory_space_constraint(out_weight, pltpu.HBM), blocks[0])
    with jax.named_scope("gather_xy"):
        mine, theirs = [], []
        for block in blocks:
            mine.append({0: block})
            for k in HOPS:
                mine[-1][k] = send(block, along_xy(k))
        mine[0][0], weight = lax.optimization_barrier((mine[0][0], weight))
        theirs.append({k: send(mine[0][k], other_core) for k in (0,) + HOPS})
        inputs = [[*(mine[0][k] for k in range(NQ)), *(theirs[0][k] for k in range(NQ))]]

    steps = 4
    at_once = lambda *n: pl.BlockSpec(n, lambda i: (0,) * len(n))
    scratch = [
        pltpu.VMEM((2 * NQ, NQ, rows * NZ, width), BF),
        pltpu.VMEM((tokens, features), BF),
    ]
    with jax.named_scope("scores"):
        raised, top = pl.pallas_call(
            scores_kernel,
            grid=(steps,),
            out_shape=(shape((vocab, tokens), F32), shape((4, tokens), F32)),
            in_specs=[VMEM] * (2 * NQ + 1),
            out_specs=(at_once(vocab, tokens), at_once(4, tokens)),
            scratch_shapes=scratch,
            cost_estimate=pl.CostEstimate(flops=0, transcendentals=0, bytes_accessed=0),
            compiler_params=pltpu.CompilerParams(vmem_limit_bytes=24 * MIB),
        )(*inputs[0], weight)
    with jax.named_scope("gather_xy"):
        theirs.append({0: send(mine[1][0], other_core)})
        held = lax.optimization_barrier((raised, *(mine[1][k] for k in HOPS)))
        raised = held[0]
        for k, piece in zip(HOPS, held[1:]):
            mine[1][k] = piece
            theirs[1][k] = send(piece, other_core)
        inputs.append([*(mine[1][k] for k in range(NQ)), *(theirs[1][k] for k in range(NQ))])
    with jax.named_scope("slopes"):
        slopes, stats = pl.pallas_call(
            slopes_kernel,
            grid=(steps,),
            out_shape=(shape((vocab, tokens), F32), shape((2 * NQ, 4, tokens), F32)),
            in_specs=[VMEM] * (2 * NQ + 3),
            out_specs=(at_once(vocab, tokens), at_once(2 * NQ, 4, tokens)),
            scratch_shapes=scratch,
            compiler_params=pltpu.CompilerParams(vmem_limit_bytes=24 * MIB),
        )(raised, top, *inputs[1], weight)

    with jax.named_scope("statistics"):
        stats = pl.pallas_call(
            merge_kernel,
            out_shape=shape((NZ * NQ, 4, tokens), F32),
            in_specs=[VMEM],
            out_specs=VMEM,
            compiler_params=pltpu.CompilerParams(vmem_limit_bytes=4 * MIB),
        )(all_of(stats, ("x", "c")))
        parts = all_of(stats, ("z", "y"))

    with jax.named_scope("product"):
        give, mixture = pl.pallas_call(
            give_kernel,
            out_shape=(
                shape((NQ, NQ, rows * NZ, width), BF),
                shape((tokens, vocab), BF),
            ),
            in_specs=[VMEM] * 5,
            out_specs=(VMEM, VMEM),
            compiler_params=pltpu.CompilerParams(vmem_limit_bytes=16 * MIB),
        )(parts, top, raised, slopes, weight)
        got = send(give, other_core)
        keep = pl.pallas_call(
            keep_kernel,
            out_shape=shape((NQ, NQ, rows * NZ, width), F32),
            in_specs=[VMEM] * 2,
            out_specs=VMEM,
            cost_estimate=pl.CostEstimate(
                flops=vocab * tokens * features,
                transcendentals=0,
                bytes_accessed=2 * vocab * features,
            ),
            compiler_params=pltpu.CompilerParams(vmem_limit_bytes=16 * MIB),
        )(mixture, weight)

    with jax.named_scope("scatter_xy"):
        sums = [keep[k] + got[k].astype(F32) for k in range(NQ)]
        total = sums[0]
        for k in HOPS:
            total = total + send(sums[k].astype(BF), along_xy(k)).astype(F32)
    with jax.named_scope("scatter_yx"):
        total, rest = total[0], total
        for k in HOPS:
            total = total + send(rest[k].astype(BF), along_yx(k)).astype(F32)
    with jax.named_scope("scatter_z"):
        return jnp.sum(all_of(total.reshape(NZ, rows, width), "z"), axis=0)


def solution(mesh):
    fine = Mesh(mesh.devices.reshape(NZ, NQ, NQ, 2), AXES)
    tokens = P(("z", "y"), ("x", "c"))
    return jax.shard_map(
        per_device,
        mesh=fine,
        in_specs=(tokens, tokens, P(AXES, None)),
        out_specs=tokens,
        check_vma=False,
    )
```

```python
import functools

import jax
import jax.numpy as jnp
from jax import lax
from jax.experimental import pallas as pl
from jax.experimental.pallas import tpu as pltpu
from jax.sharding import Mesh, PartitionSpec as P

AXES = ("z", "y", "x", "c")
BF = jnp.bfloat16
F32 = jnp.float32
VMEM = pl.BlockSpec(memory_space=pltpu.VMEM)
ANY = pl.BlockSpec(memory_space=pl.ANY)
MIB = 1024 * 1024
NZ, NQ = 8, 4


def perm(move):
    pairs = []
    for z in range(NZ):
        for y in range(NQ):
            for x in range(NQ):
                for c in range(2):
                    tz, ty, tx, tc = move(z, y, x, c)
                    src = ((z * NQ + y) * NQ + x) * 2 + c
                    dst = ((tz % NZ * NQ + ty % NQ) * NQ + tx % NQ) * 2 + tc
                    pairs.append((src, dst))
    return pairs


def send(value, move):
    return lax.ppermute(value, AXES, perm(move))


def along_yx(k):
    return lambda z, y, x, c: (z, y + k, x, c) if c == 0 else (z, y, x + k, c)


def along_xy(k):
    return lambda z, y, x, c: (z, y, x + k, c) if c == 0 else (z, y + k, x, c)


def other_core(z, y, x, c):
    return (z, y, x, 1 - c)


HOPS = (1, 3, 2)


def all_of(value, axes):
    return lax.all_to_all(value, axes, 0, 0)


def load_kernel(w, _, out, sem):
    copy = pltpu.make_async_copy(w, out, sem)
    copy.start()
    copy.wait()


def scores_kernel(*refs):
    own, theirs = refs[:5], refs[5:10]
    w, scores, slopes, stats, tops, held, whole = refs[10:]
    step = pl.program_id(0)
    rows = w.shape[0] // pl.num_programs(0)
    tokens = scores.shape[1]
    width = held.shape[-1]

    @pl.when(step == 0)
    def _():
        y, x, c = lax.axis_index("y"), lax.axis_index("x"), lax.axis_index("c")
        for pieces, parity in ((own, c), (theirs, 1 - c)):
            for k in range(NQ):
                for r in range(NQ):
                    x_back = jnp.where(parity == 0, k, r)
                    y_back = jnp.where(parity == 0, r, k)
                    x_at = lax.rem(x + NQ - x_back, NQ)
                    y_at = lax.rem(y + NQ - y_back, NQ)
                    for half in range(2):
                        piece = pieces[3 + half][r] if k == 2 else pieces[k % 3 + k // 3 * 2][half, r]
                        held[2 * x_at + parity, half, y_at] = piece
        for t in range(2 * NQ):
            whole[:, t * width : (t + 1) * width] = held[t].reshape(2 * tokens, width)

    at = pl.ds(pl.multiple_of(step * rows, rows), rows)
    both = lax.dot_general(
        w[at, :], whole[...], (((1,), (1,)), ((), ())), preferred_element_type=F32
    )
    scores[at, :] = both[:, :tokens]
    slopes[at, :] = both[:, tokens:]

    @pl.when(step == pl.num_programs(0) - 1)
    def _():
        top = jnp.max(scores[...], axis=0, keepdims=True)
        raised = jnp.exp(scores[...] - top)
        scores[...] = raised
        total = jnp.sum(raised, axis=0, keepdims=True)
        dotted = jnp.sum(raised * slopes[...], axis=0, keepdims=True)
        own_stats = jnp.concatenate((top, total, dotted, dotted), 0)
        stats[...] = jnp.broadcast_to(own_stats[None], stats.shape)
        tops[...] = jnp.broadcast_to(top, tops.shape)


def merged(parts):
    tops = parts[:, 0]
    top = jnp.max(tops, axis=0, keepdims=True)
    scale = jnp.exp(tops - top)
    total = jnp.sum(scale * parts[:, 1], axis=0, keepdims=True)
    dotted = jnp.sum(scale * parts[:, 2], axis=0, keepdims=True)
    return top, total, dotted


def merge_kernel(parts, out):
    top, total, dotted = merged(parts[...])
    own = jnp.concatenate((top, total, dotted, dotted), 0)
    out[...] = jnp.broadcast_to(own[None], out.shape)


def part_product(mixture, w, parity, out):
    y, x = lax.axis_index("y"), lax.axis_index("x")
    width, part = out.shape[-1], out.shape[-2]
    for x_of in range(NQ):
        first = (2 * x_of + parity) * width
        start = first // 128 * 128
        stop = -(-(first + width) // 128) * 128
        product = jnp.dot(mixture[...], w[:, start:stop], preferred_element_type=F32)
        piece = product[:, first - start : first - start + width].astype(out.dtype)
        x_ahead = lax.rem(x_of + NQ - x, NQ)
        for y_of in range(NQ):
            y_ahead = lax.rem(y_of + NQ - y, NQ)
            k, r = (x_ahead, y_ahead) if parity == 0 else (y_ahead, x_ahead)
            out[k, r] = piece[y_of * part : (y_of + 1) * part]


def give_kernel(parts, own_top, raised, slopes, w, give, mixture):
    top, total, dotted = merged(parts[...])
    scale = jnp.exp(own_top[0:1, :] - top) / total
    mean = dotted / total
    mix = (raised[...] * scale) * (slopes[...] - mean)
    mixture[...] = mix.T.astype(BF)
    for parity in range(2):
        pl.when(lax.axis_index("c") != parity)(
            functools.partial(part_product, mixture, w, parity, give)
        )


def keep_kernel(mixture, w, keep):
    for parity in range(2):
        pl.when(lax.axis_index("c") == parity)(
            functools.partial(part_product, mixture, w, parity, keep)
        )


def per_device(hidden, tangent, out_weight):
    rows, width = hidden.shape
    vocab, features = out_weight.shape
    tokens = rows * NZ * NQ
    shape = jax.ShapeDtypeStruct

    with jax.named_scope("gather_z"):
        own = jnp.stack((hidden, tangent))
        block = all_of(jnp.broadcast_to(own[None], (NZ, *own.shape)), "z")
        block = block.transpose(1, 0, 2, 3).reshape(2, rows * NZ, width)
    with jax.named_scope("gather_yx"):
        pieces = {0: block}
        for k in HOPS:
            pieces[k] = send(block, along_yx(k))
        block = jnp.stack([pieces[k] for k in range(NQ)], 1)
        weight = pl.pallas_call(
            load_kernel,
            out_shape=pltpu.VMEM((vocab, features), BF),
            in_specs=[ANY, ANY],
            out_specs=VMEM,
            scratch_shapes=[pltpu.SemaphoreType.DMA],
            cost_estimate=pl.CostEstimate(
                flops=0, transcendentals=0, bytes_accessed=4 * vocab * features
            ),
            compiler_params=pltpu.CompilerParams(vmem_limit_bytes=MIB),
        )(pltpu.with_memory_space_constraint(out_weight, pltpu.HBM), block)
    with jax.named_scope("gather_xy"):
        behind, ahead = send(block, along_xy(1)), send(block, along_xy(3))
        held, weight = lax.optimization_barrier((block, weight))
        own = [held, behind, ahead, send(behind[0], along_xy(1)), send(ahead[1], along_xy(3))]
        theirs = [send(piece, other_core) for piece in own]

    steps = 4
    at_once = lambda *n: pl.BlockSpec(n, lambda i: (0,) * len(n))
    with jax.named_scope("scores"):
        raised, slopes, stats, top = pl.pallas_call(
            scores_kernel,
            grid=(steps,),
            out_shape=(
                shape((vocab, tokens), F32),
                shape((vocab, tokens), F32),
                shape((2 * NQ, 4, tokens), F32),
                shape((4, tokens), F32),
            ),
            in_specs=[VMEM] * 11,
            out_specs=(
                at_once(vocab, tokens),
                at_once(vocab, tokens),
                at_once(2 * NQ, 4, tokens),
                at_once(4, tokens),
            ),
            scratch_shapes=[
                pltpu.VMEM((2 * NQ, 2, NQ, rows * NZ, width), BF),
                pltpu.VMEM((2 * tokens, features), BF),
            ],
            compiler_params=pltpu.CompilerParams(vmem_limit_bytes=20 * MIB),
        )(*own, *theirs, weight)

    with jax.named_scope("statistics"):
        stats = pl.pallas_call(
            merge_kernel,
            out_shape=shape((NZ * NQ, 4, tokens), F32),
            in_specs=[VMEM],
            out_specs=VMEM,
            compiler_params=pltpu.CompilerParams(vmem_limit_bytes=4 * MIB),
        )(all_of(stats, ("x", "c")))
        parts = all_of(stats, ("z", "y"))

    with jax.named_scope("product"):
        give, mixture = pl.pallas_call(
            give_kernel,
            out_shape=(
                shape((NQ, NQ, rows * NZ, width), BF),
                shape((tokens, vocab), BF),
            ),
            in_specs=[VMEM] * 5,
            out_specs=(VMEM, VMEM),
            compiler_params=pltpu.CompilerParams(vmem_limit_bytes=8 * MIB),
        )(parts, top, raised, slopes, weight)
        got = send(give, other_core)
        keep = pl.pallas_call(
            keep_kernel,
            out_shape=shape((NQ, NQ, rows * NZ, width), F32),
            in_specs=[VMEM] * 2,
            out_specs=VMEM,
            cost_estimate=pl.CostEstimate(
                flops=vocab * tokens * features,
                transcendentals=0,
                bytes_accessed=2 * vocab * features,
            ),
            compiler_params=pltpu.CompilerParams(vmem_limit_bytes=8 * MIB),
        )(mixture, weight)

    with jax.named_scope("scatter_xy"):
        sums = [keep[k] + got[k].astype(F32) for k in range(NQ)]
        total = sums[0]
        for k in HOPS:
            total = total + send(sums[k].astype(BF), along_xy(k)).astype(F32)
    with jax.named_scope("scatter_yx"):
        total, rest = total[0], total
        for k in HOPS:
            total = total + send(rest[k].astype(BF), along_yx(k)).astype(F32)
    with jax.named_scope("scatter_z"):
        return jnp.sum(all_of(total.reshape(NZ, rows, width), "z"), axis=0)


def solution(mesh):
    fine = Mesh(mesh.devices.reshape(NZ, NQ, NQ, 2), AXES)
    tokens = P(("z", "y"), ("x", "c"))
    return jax.shard_map(
        per_device,
        mesh=fine,
        in_specs=(tokens, tokens, P(AXES, None)),
        out_specs=tokens,
        check_vma=False,
    )
```

```python
import functools

import jax
import jax.numpy as jnp
from jax import lax
from jax.experimental import pallas as pl
from jax.experimental.pallas import tpu as pltpu
from jax.sharding import Mesh, PartitionSpec as P

AXES = ("z", "y", "x", "c")
BF = jnp.bfloat16
F32 = jnp.float32
VMEM = pl.BlockSpec(memory_space=pltpu.VMEM)
ANY = pl.BlockSpec(memory_space=pl.ANY)
MIB = 1024 * 1024
NZ, NQ = 8, 4


def perm(move):
    pairs = []
    for z in range(NZ):
        for y in range(NQ):
            for x in range(NQ):
                for c in range(2):
                    tz, ty, tx, tc = move(z, y, x, c)
                    src = ((z * NQ + y) * NQ + x) * 2 + c
                    dst = ((tz % NZ * NQ + ty % NQ) * NQ + tx % NQ) * 2 + tc
                    pairs.append((src, dst))
    return pairs


def send(value, move):
    return lax.ppermute(value, AXES, perm(move))


def along_yx(k):
    return lambda z, y, x, c: (z, y + k, x, c) if c == 0 else (z, y, x + k, c)


def along_xy(k):
    return lambda z, y, x, c: (z, y, x + k, c) if c == 0 else (z, y + k, x, c)


def other_core(z, y, x, c):
    return (z, y, x, 1 - c)


HOPS = (1, 3, 2)


def all_of(value, axes):
    return lax.all_to_all(value, axes, 0, 0)


def turn_kernel(block, out):
    both = block[...].astype(F32)
    rows = [both[:, i].reshape(-1, both.shape[-1]) for i in range(2)]
    out[...] = jnp.concatenate(rows, 0).T.astype(BF)


def load_kernel(w, _, out, sem):
    copy = pltpu.make_async_copy(w, out, sem)
    copy.start()
    copy.wait()


def scores_kernel(*refs):
    own, theirs = refs[:5], refs[5:10]
    w, scores, slopes, stats, tops, whole = refs[10:]
    step = pl.program_id(0)
    rows = w.shape[0] // pl.num_programs(0)
    width, lanes = own[0].shape[1:]

    @pl.when(step == 0)
    def _():
        y, x, c = lax.axis_index("y"), lax.axis_index("x"), lax.axis_index("c")
        for pieces, parity in ((own, c), (theirs, 1 - c)):
            for k in range(NQ):
                for r in range(NQ):
                    x_back = jnp.where(parity == 0, k, r)
                    y_back = jnp.where(parity == 0, r, k)
                    x_at = lax.rem(x + NQ - x_back, NQ)
                    y_at = lax.rem(y + NQ - y_back, NQ)
                    if k == 2:
                        piece = pieces[3 + r // 2][r % 2]
                    else:
                        piece = pieces[k % 3 + k // 3 * 2][r]
                    first = pl.multiple_of((2 * x_at + parity) * width, width)
                    column = pl.multiple_of(y_at * lanes, lanes)
                    whole[pl.ds(first, width), pl.ds(column, lanes)] = piece

    at = pl.ds(pl.multiple_of(step * rows, rows), rows)
    both = jnp.dot(w[at, :], whole[...], preferred_element_type=F32)
    low = lax.broadcasted_iota(jnp.int32, (rows, lanes), 1) < lanes // 2
    for pair in range(NQ // 2):
        first = both[:, 2 * pair * lanes : (2 * pair + 1) * lanes]
        second = both[:, (2 * pair + 1) * lanes : (2 * pair + 2) * lanes]
        columns = slice(pair * lanes, (pair + 1) * lanes)
        scores[at, columns] = jnp.where(low, first, pltpu.roll(second, lanes // 2, 1))
        slopes[at, columns] = jnp.where(low, pltpu.roll(first, lanes // 2, 1), second)

    @pl.when(step == pl.num_programs(0) - 1)
    def _():
        top = jnp.max(scores[...], axis=0, keepdims=True)
        raised = jnp.exp(scores[...] - top)
        scores[...] = raised
        total = jnp.sum(raised, axis=0, keepdims=True)
        dotted = jnp.sum(raised * slopes[...], axis=0, keepdims=True)
        own_stats = jnp.concatenate((top, total, dotted, dotted), 0)
        stats[...] = jnp.broadcast_to(own_stats[None], stats.shape)
        tops[...] = jnp.broadcast_to(top, tops.shape)


def merged(parts):
    tops = parts[:, 0]
    top = jnp.max(tops, axis=0, keepdims=True)
    scale = jnp.exp(tops - top)
    total = jnp.sum(scale * parts[:, 1], axis=0, keepdims=True)
    dotted = jnp.sum(scale * parts[:, 2], axis=0, keepdims=True)
    return top, total, dotted


def merge_kernel(parts, out):
    top, total, dotted = merged(parts[...])
    own = jnp.concatenate((top, total, dotted, dotted), 0)
    out[...] = jnp.broadcast_to(own[None], out.shape)


def part_product(mixture, w, parity, out):
    y, x = lax.axis_index("y"), lax.axis_index("x")
    width, part = out.shape[-1], out.shape[-2]
    for x_of in range(NQ):
        first = (2 * x_of + parity) * width
        start = first // 128 * 128
        stop = -(-(first + width) // 128) * 128
        product = jnp.dot(mixture[...], w[:, start:stop], preferred_element_type=F32)
        piece = product[:, first - start : first - start + width].astype(out.dtype)
        x_ahead = lax.rem(x_of + NQ - x, NQ)
        for y_of in range(NQ):
            y_ahead = lax.rem(y_of + NQ - y, NQ)
            k, r = (x_ahead, y_ahead) if parity == 0 else (y_ahead, x_ahead)
            out[k, r] = piece[y_of * part : (y_of + 1) * part]


def give_kernel(parts, own_top, raised, slopes, w, give, mixture):
    top, total, dotted = merged(parts[...])
    scale = jnp.exp(own_top[0:1, :] - top) / total
    mean = dotted / total
    mix = (raised[...] * scale) * (slopes[...] - mean)
    mixture[...] = mix.T.astype(BF)
    for parity in range(2):
        pl.when(lax.axis_index("c") != parity)(
            functools.partial(part_product, mixture, w, parity, give)
        )


def keep_kernel(mixture, w, keep):
    for parity in range(2):
        pl.when(lax.axis_index("c") == parity)(
            functools.partial(part_product, mixture, w, parity, keep)
        )


def per_device(hidden, tangent, out_weight):
    rows, width = hidden.shape
    vocab, features = out_weight.shape
    tokens = rows * NZ * NQ
    shape = jax.ShapeDtypeStruct

    with jax.named_scope("gather_z"):
        own = jnp.stack((hidden, tangent))
        block = all_of(jnp.broadcast_to(own[None], (NZ, *own.shape)), "z")
        block = pl.pallas_call(
            turn_kernel,
            out_shape=shape((width, 2 * rows * NZ), BF),
            in_specs=[VMEM],
            out_specs=VMEM,
            compiler_params=pltpu.CompilerParams(vmem_limit_bytes=4 * MIB),
        )(block)
    with jax.named_scope("gather_yx"):
        pieces = {0: block}
        for k in HOPS:
            pieces[k] = send(block, along_yx(k))
        block = jnp.stack([pieces[k] for k in range(NQ)])
        weight = pl.pallas_call(
            load_kernel,
            out_shape=pltpu.VMEM((vocab, features), BF),
            in_specs=[ANY, ANY],
            out_specs=VMEM,
            scratch_shapes=[pltpu.SemaphoreType.DMA],
            cost_estimate=pl.CostEstimate(
                flops=0, transcendentals=0, bytes_accessed=4 * vocab * features
            ),
            compiler_params=pltpu.CompilerParams(vmem_limit_bytes=MIB),
        )(pltpu.with_memory_space_constraint(out_weight, pltpu.HBM), block)
    with jax.named_scope("gather_xy"):
        behind, ahead = send(block, along_xy(1)), send(block, along_xy(3))
        held, weight = lax.optimization_barrier((block, weight))
        own = [held, behind, ahead, send(behind[:2], along_xy(1)), send(ahead[2:], along_xy(3))]
        theirs = [send(piece, other_core) for piece in own]

    steps = 4
    at_once = lambda *n: pl.BlockSpec(n, lambda i: (0,) * len(n))
    with jax.named_scope("scores"):
        raised, slopes, stats, top = pl.pallas_call(
            scores_kernel,
            grid=(steps,),
            out_shape=(
                shape((vocab, tokens), F32),
                shape((vocab, tokens), F32),
                shape((2 * NQ, 4, tokens), F32),
                shape((4, tokens), F32),
            ),
            in_specs=[VMEM] * 11,
            out_specs=(
                at_once(vocab, tokens),
                at_once(vocab, tokens),
                at_once(2 * NQ, 4, tokens),
                at_once(4, tokens),
            ),
            scratch_shapes=[
                pltpu.VMEM((features, 2 * tokens), BF),
            ],
            compiler_params=pltpu.CompilerParams(vmem_limit_bytes=20 * MIB),
        )(*own, *theirs, weight)

    with jax.named_scope("statistics"):
        stats = pl.pallas_call(
            merge_kernel,
            out_shape=shape((NZ * NQ, 4, tokens), F32),
            in_specs=[VMEM],
            out_specs=VMEM,
            compiler_params=pltpu.CompilerParams(vmem_limit_bytes=4 * MIB),
        )(all_of(stats, ("x", "c")))
        parts = all_of(stats, ("z", "y"))

    with jax.named_scope("product"):
        give, mixture = pl.pallas_call(
            give_kernel,
            out_shape=(
                shape((NQ, NQ, rows * NZ, width), BF),
                shape((tokens, vocab), BF),
            ),
            in_specs=[VMEM] * 5,
            out_specs=(VMEM, VMEM),
            compiler_params=pltpu.CompilerParams(vmem_limit_bytes=8 * MIB),
        )(parts, top, raised, slopes, weight)
        got = send(give, other_core)
        keep = pl.pallas_call(
            keep_kernel,
            out_shape=shape((NQ, NQ, rows * NZ, width), F32),
            in_specs=[VMEM] * 2,
            out_specs=VMEM,
            cost_estimate=pl.CostEstimate(
                flops=vocab * tokens * features,
                transcendentals=0,
                bytes_accessed=2 * vocab * features,
            ),
            compiler_params=pltpu.CompilerParams(vmem_limit_bytes=8 * MIB),
        )(mixture, weight)

    with jax.named_scope("scatter_xy"):
        sums = [keep[k] + got[k].astype(F32) for k in range(NQ)]
        total = sums[0]
        for k in HOPS:
            total = total + send(sums[k].astype(BF), along_xy(k)).astype(F32)
    with jax.named_scope("scatter_yx"):
        total, rest = total[0], total
        for k in HOPS:
            total = total + send(rest[k].astype(BF), along_yx(k)).astype(F32)
    with jax.named_scope("scatter_z"):
        return jnp.sum(all_of(total.reshape(NZ, rows, width), "z"), axis=0)


def solution(mesh):
    fine = Mesh(mesh.devices.reshape(NZ, NQ, NQ, 2), AXES)
    tokens = P(("z", "y"), ("x", "c"))
    return jax.shard_map(
        per_device,
        mesh=fine,
        in_specs=(tokens, tokens, P(AXES, None)),
        out_specs=tokens,
        check_vma=False,
    )
```

```python
import functools

import jax
import jax.numpy as jnp
from jax import lax
from jax.experimental import pallas as pl
from jax.experimental.pallas import tpu as pltpu
from jax.sharding import Mesh, PartitionSpec as P

AXES = ("z", "y", "x", "c")
BF = jnp.bfloat16
F32 = jnp.float32
VMEM = pl.BlockSpec(memory_space=pltpu.VMEM)
ANY = pl.BlockSpec(memory_space=pl.ANY)
MIB = 1024 * 1024
NZ, NQ = 8, 4


def perm(move):
    pairs = []
    for z in range(NZ):
        for y in range(NQ):
            for x in range(NQ):
                for c in range(2):
                    tz, ty, tx, tc = move(z, y, x, c)
                    src = ((z * NQ + y) * NQ + x) * 2 + c
                    dst = ((tz % NZ * NQ + ty % NQ) * NQ + tx % NQ) * 2 + tc
                    pairs.append((src, dst))
    return pairs


def send(value, move):
    return lax.ppermute(value, AXES, perm(move))


def along_yx(k):
    return lambda z, y, x, c: (z, y + k, x, c) if c == 0 else (z, y, x + k, c)


def along_xy(k):
    return lambda z, y, x, c: (z, y, x + k, c) if c == 0 else (z, y + k, x, c)


def other_core(z, y, x, c):
    return (z, y, x, 1 - c)


HOPS = (1, 3, 2)
PLACE = (0, 2, 1, 3)


def all_of(value, axes):
    return lax.all_to_all(value, axes, 0, 0)


def turn_kernel(block, out):
    both = block[...].astype(F32)
    rows = [both[:, i].reshape(-1, both.shape[-1]) for i in range(2)]
    out[...] = jnp.concatenate(rows, 0).T.astype(BF)


def load_kernel(w, _, out, sem):
    copy = pltpu.make_async_copy(w, out, sem)
    copy.start()
    copy.wait()


def scores_kernel(*refs):
    own, theirs = refs[:NQ], refs[NQ : 2 * NQ]
    w, raised, slopes, stats, tops, whole = refs[2 * NQ :]
    width, lanes = own[0].shape[1:]
    y, x, c = lax.axis_index("y"), lax.axis_index("x"), lax.axis_index("c")
    for pieces, parity in ((own, c), (theirs, 1 - c)):
        for k in range(NQ):
            for r in range(NQ):
                x_back = jnp.where(parity == 0, k, r)
                y_back = jnp.where(parity == 0, r, k)
                x_at = lax.rem(x + NQ - x_back, NQ)
                y_at = lax.rem(y + NQ - y_back, NQ)
                first = pl.multiple_of((2 * x_at + parity) * width, width)
                column = pl.multiple_of(y_at * lanes, lanes)
                whole[pl.ds(first, width), pl.ds(column, lanes)] = pieces[PLACE[k]][r]

    both = jnp.dot(w[...], whole[...], preferred_element_type=F32)
    low = lax.broadcasted_iota(jnp.int32, (both.shape[0], lanes), 1) < lanes // 2
    for pair in range(NQ // 2):
        first = both[:, 2 * pair * lanes : (2 * pair + 1) * lanes]
        second = both[:, (2 * pair + 1) * lanes : (2 * pair + 2) * lanes]
        columns = slice(pair * lanes, (pair + 1) * lanes)
        raised[:, columns] = jnp.where(low, first, pltpu.roll(second, lanes // 2, 1))
        slopes[:, columns] = jnp.where(low, pltpu.roll(first, lanes // 2, 1), second)

    top = jnp.max(raised[...], axis=0, keepdims=True)
    value = jnp.exp(raised[...] - top)
    raised[...] = value
    total = jnp.sum(value, axis=0, keepdims=True)
    dotted = jnp.sum(value * slopes[...], axis=0, keepdims=True)
    own_stats = jnp.concatenate((top, total, dotted, dotted), 0)
    stats[...] = jnp.broadcast_to(own_stats[None], stats.shape)
    tops[...] = jnp.broadcast_to(top, tops.shape)


def merged(parts):
    tops = parts[:, 0]
    top = jnp.max(tops, axis=0, keepdims=True)
    scale = jnp.exp(tops - top)
    total = jnp.sum(scale * parts[:, 1], axis=0, keepdims=True)
    dotted = jnp.sum(scale * parts[:, 2], axis=0, keepdims=True)
    return top, total, dotted


def merge_kernel(parts, out):
    top, total, dotted = merged(parts[...])
    own = jnp.concatenate((top, total, dotted, dotted), 0)
    out[...] = jnp.broadcast_to(own[None], out.shape)


def part_product(mixture, w, parity, out):
    y, x = lax.axis_index("y"), lax.axis_index("x")
    width, part = out.shape[-1], out.shape[-2]
    for x_of in range(NQ):
        first = (2 * x_of + parity) * width
        start = first // 128 * 128
        stop = -(-(first + width) // 128) * 128
        product = jnp.dot(mixture[...], w[:, start:stop], preferred_element_type=F32)
        piece = product[:, first - start : first - start + width].astype(out.dtype)
        x_ahead = lax.rem(x_of + NQ - x, NQ)
        for y_of in range(NQ):
            y_ahead = lax.rem(y_of + NQ - y, NQ)
            k, r = (x_ahead, y_ahead) if parity == 0 else (y_ahead, x_ahead)
            out[k, r] = piece[y_of * part : (y_of + 1) * part]


def give_kernel(parts, own_top, raised, slopes, w, give, mixture):
    top, total, dotted = merged(parts[...])
    scale = jnp.exp(own_top[0:1, :] - top) / total
    mean = dotted / total
    mix = (raised[...] * scale) * (slopes[...] - mean)
    mixture[...] = mix.T.astype(BF)
    for parity in range(2):
        pl.when(lax.axis_index("c") != parity)(
            functools.partial(part_product, mixture, w, parity, give)
        )


def keep_kernel(mixture, w, keep):
    for parity in range(2):
        pl.when(lax.axis_index("c") == parity)(
            functools.partial(part_product, mixture, w, parity, keep)
        )


def per_device(hidden, tangent, out_weight):
    rows, width = hidden.shape
    vocab, features = out_weight.shape
    tokens = rows * NZ * NQ
    shape = jax.ShapeDtypeStruct

    with jax.named_scope("gather_z"):
        own = jnp.stack((hidden, tangent))
        block = all_of(jnp.broadcast_to(own[None], (NZ, *own.shape)), "z")
        block = pl.pallas_call(
            turn_kernel,
            out_shape=shape((width, 2 * rows * NZ), BF),
            in_specs=[VMEM],
            out_specs=VMEM,
            compiler_params=pltpu.CompilerParams(vmem_limit_bytes=4 * MIB),
        )(block)
    with jax.named_scope("gather_yx"):
        pieces = {0: block}
        for k in HOPS:
            pieces[k] = send(block, along_yx(k))
        block = jnp.stack([pieces[k] for k in range(NQ)])
        weight = pl.pallas_call(
            load_kernel,
            out_shape=pltpu.VMEM((vocab, features), BF),
            in_specs=[ANY, ANY],
            out_specs=VMEM,
            scratch_shapes=[pltpu.SemaphoreType.DMA],
            cost_estimate=pl.CostEstimate(
                flops=0, transcendentals=0, bytes_accessed=4 * vocab * features
            ),
            compiler_params=pltpu.CompilerParams(vmem_limit_bytes=MIB),
        )(pltpu.with_memory_space_constraint(out_weight, pltpu.HBM), block)
    with jax.named_scope("gather_xy"):
        pieces = {0: block}
        for k in HOPS:
            pieces[k] = send(block, along_xy(k))
        pieces[0], weight = lax.optimization_barrier((pieces[0], weight))
        theirs = {k: send(pieces[k], other_core) for k in (0,) + HOPS}

    with jax.named_scope("scores"):
        raised, slopes, stats, top = pl.pallas_call(
            scores_kernel,
            out_shape=(
                shape((vocab, tokens), F32),
                shape((vocab, tokens), F32),
                shape((NQ * NQ, 4, tokens), F32),
                shape((4, tokens), F32),
            ),
            in_specs=[VMEM] * (2 * NQ + 1),
            out_specs=(VMEM,) * 4,
            scratch_shapes=[pltpu.VMEM((features, 2 * tokens), BF)],
            compiler_params=pltpu.CompilerParams(vmem_limit_bytes=20 * MIB),
        )(*(pieces[k] for k in PLACE), *(theirs[k] for k in PLACE), weight)

    with jax.named_scope("statistics"):
        stats = pl.pallas_call(
            merge_kernel,
            out_shape=shape((2 * NZ, 4, tokens), F32),
            in_specs=[VMEM],
            out_specs=VMEM,
            compiler_params=pltpu.CompilerParams(vmem_limit_bytes=4 * MIB),
        )(all_of(stats, ("y", "x")))
        parts = all_of(stats, ("z", "c"))

    with jax.named_scope("product"):
        give, mixture = pl.pallas_call(
            give_kernel,
            out_shape=(
                shape((NQ, NQ, rows * NZ, width), BF),
                shape((tokens, vocab), BF),
            ),
            in_specs=[VMEM] * 5,
            out_specs=(VMEM, VMEM),
            compiler_params=pltpu.CompilerParams(vmem_limit_bytes=8 * MIB),
        )(parts, top, raised, slopes, weight)
        got = send(give, other_core)
        keep = pl.pallas_call(
            keep_kernel,
            out_shape=shape((NQ, NQ, rows * NZ, width), F32),
            in_specs=[VMEM] * 2,
            out_specs=VMEM,
            cost_estimate=pl.CostEstimate(
                flops=vocab * tokens * features,
                transcendentals=0,
                bytes_accessed=2 * vocab * features,
            ),
            compiler_params=pltpu.CompilerParams(vmem_limit_bytes=8 * MIB),
        )(mixture, weight)

    with jax.named_scope("scatter_xy"):
        sums = [keep[k] + got[k].astype(F32) for k in range(NQ)]
        total = sums[0]
        for k in HOPS:
            total = total + send(sums[k].astype(BF), along_xy(k)).astype(F32)
    with jax.named_scope("scatter_yx"):
        total, rest = total[0], total
        for k in HOPS:
            total = total + send(rest[k].astype(BF), along_yx(k)).astype(F32)
    with jax.named_scope("scatter_z"):
        return jnp.sum(all_of(total.reshape(NZ, rows, width), "z"), axis=0)


def solution(mesh):
    fine = Mesh(mesh.devices.reshape(NZ, NQ, NQ, 2), AXES)
    tokens = P(("z", "y"), ("x", "c"))
    return jax.shard_map(
        per_device,
        mesh=fine,
        in_specs=(tokens, tokens, P(AXES, None)),
        out_specs=tokens,
        check_vma=False,
    )
```

```python
import functools

import jax
import jax.numpy as jnp
from jax import lax
from jax.experimental import pallas as pl
from jax.experimental.pallas import tpu as pltpu
from jax.sharding import Mesh, PartitionSpec as P

AXES = ("z", "y", "x", "c")
BF = jnp.bfloat16
F32 = jnp.float32
VMEM = pl.BlockSpec(memory_space=pltpu.VMEM)
ANY = pl.BlockSpec(memory_space=pl.ANY)
MIB = 1024 * 1024
NZ, NQ = 8, 4


def perm(move):
    pairs = []
    for z in range(NZ):
        for y in range(NQ):
            for x in range(NQ):
                for c in range(2):
                    tz, ty, tx, tc = move(z, y, x, c)
                    src = ((z * NQ + y) * NQ + x) * 2 + c
                    dst = ((tz % NZ * NQ + ty % NQ) * NQ + tx % NQ) * 2 + tc
                    pairs.append((src, dst))
    return pairs


def send(value, move):
    return lax.ppermute(value, AXES, perm(move))


def along_x(k):
    return lambda z, y, x, c: (z, y, x + k, c)


def along_yx(k):
    return lambda z, y, x, c: (z, y + k, x, c) if c == 0 else (z, y, x + k, c)


def along_xy(k):
    return lambda z, y, x, c: (z, y, x + k, c) if c == 0 else (z, y + k, x, c)


def other_core(z, y, x, c):
    return (z, y, x, 1 - c)


HOPS = (1, 3, 2)


def all_of(value, axes):
    return lax.all_to_all(value, axes, 0, 0)


def turn_kernel(block, out):
    both = block[...].astype(F32)
    rows = [both[:, i].reshape(-1, both.shape[-1]) for i in range(2)]
    out[...] = jnp.concatenate(rows, 0).T.astype(BF)


def load_kernel(w, _, out, sem):
    copy = pltpu.make_async_copy(w, out, sem)
    copy.start()
    copy.wait()


def scores_kernel(*refs):
    own, theirs = refs[:5], refs[5:10]
    w, raised, slopes, stats, whole = refs[10:]
    width, lanes = own[0].shape[1:]
    y, x, c = lax.axis_index("y"), lax.axis_index("x"), lax.axis_index("c")
    for pieces, parity in ((own, c), (theirs, 1 - c)):
        for k in range(NQ):
            for r in range(NQ):
                x_back = jnp.where(parity == 0, k, r)
                y_back = jnp.where(parity == 0, r, k)
                x_at = lax.rem(x + NQ - x_back, NQ)
                y_at = lax.rem(y + NQ - y_back, NQ)
                first = pl.multiple_of((2 * x_at + parity) * width, width)
                column = pl.multiple_of(y_at * lanes, lanes)
                same, near, far, behind, ahead = pieces
                if k == 0:
                    piece = same[r]
                elif k == 2:
                    piece = (near, far)[r // 2][r % 2]
                elif r == 0:
                    piece = same[NQ + k // 2]
                else:
                    piece = (behind, ahead)[k // 2][r - 1]
                whole[pl.ds(first, width), pl.ds(column, lanes)] = piece

    both = jnp.dot(w[...], whole[...], preferred_element_type=F32)
    low = lax.broadcasted_iota(jnp.int32, (both.shape[0], lanes), 1) < lanes // 2
    for pair in range(NQ // 2):
        first = both[:, 2 * pair * lanes : (2 * pair + 1) * lanes]
        second = both[:, (2 * pair + 1) * lanes : (2 * pair + 2) * lanes]
        columns = slice(pair * lanes, (pair + 1) * lanes)
        raised[:, columns] = jnp.where(low, first, pltpu.roll(second, lanes // 2, 1))
        slopes[:, columns] = jnp.where(low, pltpu.roll(first, lanes // 2, 1), second)

    top = jnp.max(raised[...], axis=0, keepdims=True)
    value = jnp.exp(raised[...] - top)
    raised[...] = value
    total = jnp.sum(value, axis=0, keepdims=True)
    dotted = jnp.sum(value * slopes[...], axis=0, keepdims=True)
    stats[...] = jnp.concatenate((top, total, dotted, dotted), 0)


def merged(parts):
    tops = parts[:, 0]
    top = jnp.max(tops, axis=0, keepdims=True)
    scale = jnp.exp(tops - top)
    total = jnp.sum(scale * parts[:, 1], axis=0, keepdims=True)
    dotted = jnp.sum(scale * parts[:, 2], axis=0, keepdims=True)
    return top, total, dotted


def merge_kernel(*refs):
    *parts, out = refs
    top, total, dotted = merged(jnp.stack([part[...] for part in parts]))
    own = jnp.concatenate((top, total, dotted, dotted), 0)
    out[...] = jnp.broadcast_to(own, out.shape)


def part_product(mixture, w, parity, out):
    y, x = lax.axis_index("y"), lax.axis_index("x")
    width, part = out.shape[-1], out.shape[-2]
    for x_of in range(NQ):
        first = (2 * x_of + parity) * width
        start = first // 128 * 128
        stop = -(-(first + width) // 128) * 128
        product = jnp.dot(mixture[...], w[:, start:stop], preferred_element_type=F32)
        piece = product[:, first - start : first - start + width].astype(out.dtype)
        x_ahead = lax.rem(x_of + NQ - x, NQ)
        for y_of in range(NQ):
            y_ahead = lax.rem(y_of + NQ - y, NQ)
            k, r = (x_ahead, y_ahead) if parity == 0 else (y_ahead, x_ahead)
            out[k, r] = piece[y_of * part : (y_of + 1) * part]


def give_kernel(parts, own_top, raised, slopes, w, give, mixture):
    top, total, dotted = merged(parts[...])
    scale = jnp.exp(own_top[0:1, :] - top) / total
    mean = dotted / total
    mix = (raised[...] * scale) * (slopes[...] - mean)
    mixture[...] = mix.T.astype(BF)
    for parity in range(2):
        pl.when(lax.axis_index("c") != parity)(
            functools.partial(part_product, mixture, w, parity, give)
        )


def keep_kernel(mixture, w, keep):
    for parity in range(2):
        pl.when(lax.axis_index("c") == parity)(
            functools.partial(part_product, mixture, w, parity, keep)
        )


def per_device(hidden, tangent, out_weight):
    rows, width = hidden.shape
    vocab, features = out_weight.shape
    tokens = rows * NZ * NQ
    shape = jax.ShapeDtypeStruct

    with jax.named_scope("gather_z"):
        own = jnp.stack((hidden, tangent))
        block = all_of(jnp.broadcast_to(own[None], (NZ, *own.shape)), "z")
        block = pl.pallas_call(
            turn_kernel,
            out_shape=shape((width, 2 * rows * NZ), BF),
            in_specs=[VMEM],
            out_specs=VMEM,
            compiler_params=pltpu.CompilerParams(vmem_limit_bytes=4 * MIB),
        )(block)
    with jax.named_scope("gather_yx"):
        pieces = {k: send(block, along_yx(k)) for k in HOPS}
        early = [send(block, along_xy(k)) for k in (1, 3)]
        pieces[1], *early = lax.optimization_barrier((pieces[1], *early))
        late = jnp.stack([pieces[k] for k in range(1, NQ)])
        weight = pl.pallas_call(
            load_kernel,
            out_shape=pltpu.VMEM((vocab, features), BF),
            in_specs=[ANY, ANY],
            out_specs=VMEM,
            scratch_shapes=[pltpu.SemaphoreType.DMA],
            cost_estimate=pl.CostEstimate(
                flops=0, transcendentals=0, bytes_accessed=4 * vocab * features
            ),
            compiler_params=pltpu.CompilerParams(vmem_limit_bytes=MIB),
        )(pltpu.with_memory_space_constraint(out_weight, pltpu.HBM), late)
    with jax.named_scope("gather_xy"):
        behind, ahead = send(late, along_xy(1)), send(late, along_xy(3))
        pieces[0] = block
        across = [send(jnp.stack((pieces[k], pieces[k + 1])), along_xy(2)) for k in (0, 2)]
        same = jnp.stack((*(pieces[k] for k in range(NQ)), *early))
        same, weight = lax.optimization_barrier((same, weight))
        own = [same, *across, behind, ahead]
        theirs = [send(piece, other_core) for piece in own]

    with jax.named_scope("scores"):
        raised, slopes, mine = pl.pallas_call(
            scores_kernel,
            out_shape=(
                shape((vocab, tokens), F32),
                shape((vocab, tokens), F32),
                shape((4, tokens), F32),
            ),
            in_specs=[VMEM] * 11,
            out_specs=(VMEM,) * 3,
            scratch_shapes=[pltpu.VMEM((features, 2 * tokens), BF)],
            compiler_params=pltpu.CompilerParams(vmem_limit_bytes=20 * MIB),
        )(*own, *theirs, weight)

    with jax.named_scope("statistics"):

        def merge(parts, *copies):
            return pl.pallas_call(
                merge_kernel,
                out_shape=shape((*copies, 4, tokens), F32),
                in_specs=[VMEM] * len(parts),
                out_specs=VMEM,
                compiler_params=pltpu.CompilerParams(vmem_limit_bytes=4 * MIB),
            )(*parts)

        chip = merge([mine, send(mine, other_core)])
        row = merge([chip, *(send(chip, along_x(k)) for k in HOPS)], NZ * NQ)
        parts = all_of(row, ("z", "y"))

    with jax.named_scope("product"):
        give, mixture = pl.pallas_call(
            give_kernel,
            out_shape=(
                shape((NQ, NQ, rows * NZ, width), BF),
                shape((tokens, vocab), BF),
            ),
            in_specs=[VMEM] * 5,
            out_specs=(VMEM, VMEM),
            compiler_params=pltpu.CompilerParams(vmem_limit_bytes=8 * MIB),
        )(parts, mine, raised, slopes, weight)
        got = send(give, other_core)
        keep = pl.pallas_call(
            keep_kernel,
            out_shape=shape((NQ, NQ, rows * NZ, width), F32),
            in_specs=[VMEM] * 2,
            out_specs=VMEM,
            cost_estimate=pl.CostEstimate(
                flops=vocab * tokens * features,
                transcendentals=0,
                bytes_accessed=2 * vocab * features,
            ),
            compiler_params=pltpu.CompilerParams(vmem_limit_bytes=8 * MIB),
        )(mixture, weight)

    with jax.named_scope("scatter_xy"):
        sums = [keep[k] + got[k].astype(F32) for k in range(NQ)]
        total = sums[0]
        for k in HOPS:
            total = total + send(sums[k].astype(BF), along_xy(k)).astype(F32)
    with jax.named_scope("scatter_yx"):
        total, rest = total[0], total
        for k in HOPS:
            total = total + send(rest[k].astype(BF), along_yx(k)).astype(F32)
    with jax.named_scope("scatter_z"):
        return jnp.sum(all_of(total.reshape(NZ, rows, width), "z"), axis=0)


def solution(mesh):
    fine = Mesh(mesh.devices.reshape(NZ, NQ, NQ, 2), AXES)
    tokens = P(("z", "y"), ("x", "c"))
    return jax.shard_map(
        per_device,
        mesh=fine,
        in_specs=(tokens, tokens, P(AXES, None)),
        out_specs=tokens,
        check_vma=False,
    )
```

```python
import functools

import jax
import jax.numpy as jnp
from jax import lax
from jax.experimental import pallas as pl
from jax.experimental.pallas import tpu as pltpu
from jax.sharding import Mesh, PartitionSpec as P

AXES = ("z", "y", "x", "c")
BF = jnp.bfloat16
F32 = jnp.float32
VMEM = pl.BlockSpec(memory_space=pltpu.VMEM)
ANY = pl.BlockSpec(memory_space=pl.ANY)
MIB = 1024 * 1024
NZ, NQ = 8, 4


def perm(move):
    pairs = []
    for z in range(NZ):
        for y in range(NQ):
            for x in range(NQ):
                for c in range(2):
                    tz, ty, tx, tc = move(z, y, x, c)
                    src = ((z * NQ + y) * NQ + x) * 2 + c
                    dst = ((tz % NZ * NQ + ty % NQ) * NQ + tx % NQ) * 2 + tc
                    pairs.append((src, dst))
    return pairs


def send(value, move):
    return lax.ppermute(value, AXES, perm(move))


def along_yx(k):
    return lambda z, y, x, c: (z, y + k, x, c) if c == 0 else (z, y, x + k, c)


def along_xy(k):
    return lambda z, y, x, c: (z, y, x + k, c) if c == 0 else (z, y + k, x, c)


def other_core(z, y, x, c):
    return (z, y, x, 1 - c)


HOPS = (1, 3, 2)


def all_of(value, axes):
    return lax.all_to_all(value, axes, 0, 0)


def turn_kernel(block, out):
    both = block[...].astype(F32)
    rows = [both[:, i].reshape(-1, both.shape[-1]) for i in range(2)]
    out[...] = jnp.concatenate(rows, 0).T.astype(BF)


def load_kernel(w, _, out, sem):
    copy = pltpu.make_async_copy(w, out, sem)
    copy.start()
    copy.wait()


def scores_kernel(*refs):
    own, theirs = refs[:5], refs[5:10]
    w, raised, slopes, stats, tops, whole = refs[10:]
    width, lanes = own[0].shape[1:]
    y, x, c = lax.axis_index("y"), lax.axis_index("x"), lax.axis_index("c")
    for pieces, parity in ((own, c), (theirs, 1 - c)):
        for k in range(NQ):
            for r in range(NQ):
                x_back = jnp.where(parity == 0, k, r)
                y_back = jnp.where(parity == 0, r, k)
                x_at = lax.rem(x + NQ - x_back, NQ)
                y_at = lax.rem(y + NQ - y_back, NQ)
                first = pl.multiple_of((2 * x_at + parity) * width, width)
                column = pl.multiple_of(y_at * lanes, lanes)
                far, near, behind, ahead, same = pieces
                if k == 2:
                    piece = (near, far)[r // 2][r % 2]
                else:
                    piece = (same, behind, None, ahead)[k][r]
                whole[pl.ds(first, width), pl.ds(column, lanes)] = piece

    both = jnp.dot(w[...], whole[...], preferred_element_type=F32)
    low = lax.broadcasted_iota(jnp.int32, (both.shape[0], lanes), 1) < lanes // 2
    for pair in range(NQ // 2):
        first = both[:, 2 * pair * lanes : (2 * pair + 1) * lanes]
        second = both[:, (2 * pair + 1) * lanes : (2 * pair + 2) * lanes]
        columns = slice(pair * lanes, (pair + 1) * lanes)
        raised[:, columns] = jnp.where(low, first, pltpu.roll(second, lanes // 2, 1))
        slopes[:, columns] = jnp.where(low, pltpu.roll(first, lanes // 2, 1), second)

    top = jnp.max(raised[...], axis=0, keepdims=True)
    value = jnp.exp(raised[...] - top)
    raised[...] = value
    total = jnp.sum(value, axis=0, keepdims=True)
    dotted = jnp.sum(value * slopes[...], axis=0, keepdims=True)
    own_stats = jnp.concatenate((top, total, dotted, dotted), 0)
    stats[...] = jnp.broadcast_to(own_stats[None], stats.shape)
    tops[...] = jnp.broadcast_to(top, tops.shape)


def merged(parts):
    tops = parts[:, 0]
    top = jnp.max(tops, axis=0, keepdims=True)
    scale = jnp.exp(tops - top)
    total = jnp.sum(scale * parts[:, 1], axis=0, keepdims=True)
    dotted = jnp.sum(scale * parts[:, 2], axis=0, keepdims=True)
    return top, total, dotted


def merge_kernel(parts, out):
    top, total, dotted = merged(parts[...])
    own = jnp.concatenate((top, total, dotted, dotted), 0)
    out[...] = jnp.broadcast_to(own[None], out.shape)


def part_product(mixture, w, parity, out):
    y, x = lax.axis_index("y"), lax.axis_index("x")
    width, part = out.shape[-1], out.shape[-2]
    for x_of in range(NQ):
        first = (2 * x_of + parity) * width
        start = first // 128 * 128
        stop = -(-(first + width) // 128) * 128
        product = jnp.dot(mixture[...], w[:, start:stop], preferred_element_type=F32)
        piece = product[:, first - start : first - start + width].astype(out.dtype)
        x_ahead = lax.rem(x_of + NQ - x, NQ)
        for y_of in range(NQ):
            y_ahead = lax.rem(y_of + NQ - y, NQ)
            k, r = (x_ahead, y_ahead) if parity == 0 else (y_ahead, x_ahead)
            out[k, r] = piece[y_of * part : (y_of + 1) * part]


def give_kernel(parts, own_top, raised, slopes, w, give, mixture):
    top, total, dotted = merged(parts[...])
    scale = jnp.exp(own_top[0:1, :] - top) / total
    mean = dotted / total
    mix = (raised[...] * scale) * (slopes[...] - mean)
    mixture[...] = mix.T.astype(BF)
    for parity in range(2):
        pl.when(lax.axis_index("c") != parity)(
            functools.partial(part_product, mixture, w, parity, give)
        )


def keep_kernel(mixture, w, keep):
    for parity in range(2):
        pl.when(lax.axis_index("c") == parity)(
            functools.partial(part_product, mixture, w, parity, keep)
        )


def per_device(hidden, tangent, out_weight):
    rows, width = hidden.shape
    vocab, features = out_weight.shape
    tokens = rows * NZ * NQ
    shape = jax.ShapeDtypeStruct

    with jax.named_scope("gather_z"):
        own = jnp.stack((hidden, tangent))
        block = all_of(jnp.broadcast_to(own[None], (NZ, *own.shape)), "z")
        block = pl.pallas_call(
            turn_kernel,
            out_shape=shape((width, 2 * rows * NZ), BF),
            in_specs=[VMEM],
            out_specs=VMEM,
            compiler_params=pltpu.CompilerParams(vmem_limit_bytes=4 * MIB),
        )(block)
    with jax.named_scope("gather_yx"):
        pieces = {0: block}
        for k in HOPS:
            pieces[k] = send(block, along_yx(k))
        block = jnp.stack([pieces[k] for k in range(NQ)])
        weight = pl.pallas_call(
            load_kernel,
            out_shape=pltpu.VMEM((vocab, features), BF),
            in_specs=[ANY, ANY],
            out_specs=VMEM,
            scratch_shapes=[pltpu.SemaphoreType.DMA],
            cost_estimate=pl.CostEstimate(
                flops=0, transcendentals=0, bytes_accessed=4 * vocab * features
            ),
            compiler_params=pltpu.CompilerParams(vmem_limit_bytes=MIB),
        )(pltpu.with_memory_space_constraint(out_weight, pltpu.HBM), block)
    with jax.named_scope("gather_xy"):
        ahead = send(block, along_xy(3))
        near = send(block[: NQ // 2], along_xy(2))
        behind = send(block, along_xy(1))
        far = send(ahead[NQ // 2 :], along_xy(3))
        same, weight = lax.optimization_barrier((block, weight))
        own = [far, near, behind, ahead, same]
        theirs = [send(piece, other_core) for piece in own]

    with jax.named_scope("scores"):
        raised, slopes, stats, top = pl.pallas_call(
            scores_kernel,
            out_shape=(
                shape((vocab, tokens), F32),
                shape((vocab, tokens), F32),
                shape((NQ * NQ, 4, tokens), F32),
                shape((4, tokens), F32),
            ),
            in_specs=[VMEM] * 11,
            out_specs=(VMEM,) * 4,
            scratch_shapes=[pltpu.VMEM((features, 2 * tokens), BF)],
            compiler_params=pltpu.CompilerParams(vmem_limit_bytes=20 * MIB),
        )(*own, *theirs, weight)

    with jax.named_scope("statistics"):
        stats = pl.pallas_call(
            merge_kernel,
            out_shape=shape((2 * NZ, 4, tokens), F32),
            in_specs=[VMEM],
            out_specs=VMEM,
            compiler_params=pltpu.CompilerParams(vmem_limit_bytes=4 * MIB),
        )(all_of(stats, ("y", "x")))
        parts = all_of(stats, ("z", "c"))

    with jax.named_scope("product"):
        give, mixture = pl.pallas_call(
            give_kernel,
            out_shape=(
                shape((NQ, NQ, rows * NZ, width), BF),
                shape((tokens, vocab), BF),
            ),
            in_specs=[VMEM] * 5,
            out_specs=(VMEM, VMEM),
            compiler_params=pltpu.CompilerParams(vmem_limit_bytes=8 * MIB),
        )(parts, top, raised, slopes, weight)
        got = send(give, other_core)
        keep = pl.pallas_call(
            keep_kernel,
            out_shape=shape((NQ, NQ, rows * NZ, width), F32),
            in_specs=[VMEM] * 2,
            out_specs=VMEM,
            cost_estimate=pl.CostEstimate(
                flops=vocab * tokens * features,
                transcendentals=0,
                bytes_accessed=2 * vocab * features,
            ),
            compiler_params=pltpu.CompilerParams(vmem_limit_bytes=8 * MIB),
        )(mixture, weight)

    with jax.named_scope("scatter_xy"):
        sums = [keep[k] + got[k].astype(F32) for k in range(NQ)]
        total = sums[0]
        for k in HOPS:
            total = total + send(sums[k].astype(BF), along_xy(k)).astype(F32)
    with jax.named_scope("scatter_yx"):
        total, rest = total[0], total
        for k in HOPS:
            total = total + send(rest[k].astype(BF), along_yx(k)).astype(F32)
    with jax.named_scope("scatter_z"):
        return jnp.sum(all_of(total.reshape(NZ, rows, width), "z"), axis=0)


def solution(mesh):
    fine = Mesh(mesh.devices.reshape(NZ, NQ, NQ, 2), AXES)
    tokens = P(("z", "y"), ("x", "c"))
    return jax.shard_map(
        per_device,
        mesh=fine,
        in_specs=(tokens, tokens, P(AXES, None)),
        out_specs=tokens,
        check_vma=False,
    )
```

```python
import functools

import jax
import jax.numpy as jnp
from jax import lax
from jax.experimental import pallas as pl
from jax.experimental.pallas import tpu as pltpu
from jax.sharding import Mesh, PartitionSpec as P

AXES = ("z", "y", "x", "c")
BF = jnp.bfloat16
F32 = jnp.float32
VMEM = pl.BlockSpec(memory_space=pltpu.VMEM)
ANY = pl.BlockSpec(memory_space=pl.ANY)
MIB = 1024 * 1024
NZ, NQ = 8, 4


def perm(move):
    pairs = []
    for z in range(NZ):
        for y in range(NQ):
            for x in range(NQ):
                for c in range(2):
                    tz, ty, tx, tc = move(z, y, x, c)
                    src = ((z * NQ + y) * NQ + x) * 2 + c
                    dst = ((tz % NZ * NQ + ty % NQ) * NQ + tx % NQ) * 2 + tc
                    pairs.append((src, dst))
    return pairs


def send(value, move):
    return lax.ppermute(value, AXES, perm(move))


def along_yx(k):
    return lambda z, y, x, c: (z, y + k, x, c) if c == 0 else (z, y, x + k, c)


def along_xy(k):
    return lambda z, y, x, c: (z, y, x + k, c) if c == 0 else (z, y + k, x, c)


def other_core(z, y, x, c):
    return (z, y, x, 1 - c)


HOPS = (1, 3, 2)
BACK_HOPS = (2, 3, 1)


def all_of(value, axes):
    return lax.all_to_all(value, axes, 0, 0)


def turn_kernel(block, out):
    both = block[...].astype(F32)
    rows = [both[:, i].reshape(-1, both.shape[-1]) for i in range(2)]
    out[...] = jnp.concatenate(rows, 0).T.astype(BF)


def load_kernel(w, _, out, sem):
    copy = pltpu.make_async_copy(w, out, sem)
    copy.start()
    copy.wait()


def scores_kernel(*refs):
    own, theirs = refs[:5], refs[5:10]
    w, raised, slopes, stats, tops, whole = refs[10:]
    width, lanes = own[0].shape[1:]
    y, x, c = lax.axis_index("y"), lax.axis_index("x"), lax.axis_index("c")
    for pieces, parity in ((own, c), (theirs, 1 - c)):
        for k in range(NQ):
            for r in range(NQ):
                x_back = jnp.where(parity == 0, k, r)
                y_back = jnp.where(parity == 0, r, k)
                x_at = lax.rem(x + NQ - x_back, NQ)
                y_at = lax.rem(y + NQ - y_back, NQ)
                first = pl.multiple_of((2 * x_at + parity) * width, width)
                column = pl.multiple_of(y_at * lanes, lanes)
                near, far, behind, ahead, same = pieces
                if k == 2:
                    piece = (near, far)[r // 2][r % 2]
                else:
                    piece = (same, behind, None, ahead)[k][r]
                whole[pl.ds(first, width), pl.ds(column, lanes)] = piece

    both = jnp.dot(w[...], whole[...], preferred_element_type=F32)
    low = lax.broadcasted_iota(jnp.int32, (both.shape[0], lanes), 1) < lanes // 2
    for pair in range(NQ // 2):
        first = both[:, 2 * pair * lanes : (2 * pair + 1) * lanes]
        second = both[:, (2 * pair + 1) * lanes : (2 * pair + 2) * lanes]
        columns = slice(pair * lanes, (pair + 1) * lanes)
        raised[:, columns] = jnp.where(low, first, pltpu.roll(second, lanes // 2, 1))
        slopes[:, columns] = jnp.where(low, pltpu.roll(first, lanes // 2, 1), second)

    top = jnp.max(raised[...], axis=0, keepdims=True)
    value = jnp.exp(raised[...] - top)
    raised[...] = value
    total = jnp.sum(value, axis=0, keepdims=True)
    dotted = jnp.sum(value * slopes[...], axis=0, keepdims=True)
    own_stats = jnp.concatenate((top, total, dotted, dotted), 0)
    stats[...] = jnp.broadcast_to(own_stats[None], stats.shape)
    tops[...] = jnp.broadcast_to(top, tops.shape)


def merged(parts):
    tops = parts[:, 0]
    top = jnp.max(tops, axis=0, keepdims=True)
    scale = jnp.exp(tops - top)
    total = jnp.sum(scale * parts[:, 1], axis=0, keepdims=True)
    dotted = jnp.sum(scale * parts[:, 2], axis=0, keepdims=True)
    return top, total, dotted


def merge_kernel(parts, out):
    top, total, dotted = merged(parts[...])
    own = jnp.concatenate((top, total, dotted, dotted), 0)
    out[...] = jnp.broadcast_to(own[None], out.shape)


def part_product(mixture, w, parity, out):
    y, x = lax.axis_index("y"), lax.axis_index("x")
    width, part = out.shape[-1], out.shape[-2]
    for x_of in range(NQ):
        first = (2 * x_of + parity) * width
        start = first // 128 * 128
        stop = -(-(first + width) // 128) * 128
        product = jnp.dot(mixture[...], w[:, start:stop], preferred_element_type=F32)
        piece = product[:, first - start : first - start + width].astype(out.dtype)
        x_ahead = lax.rem(x_of + NQ - x, NQ)
        for y_of in range(NQ):
            y_ahead = lax.rem(y_of + NQ - y, NQ)
            k, r = (x_ahead, y_ahead) if parity == 0 else (y_ahead, x_ahead)
            out[k, r] = piece[y_of * part : (y_of + 1) * part]


def give_kernel(parts, own_top, raised, slopes, w, give, mixture):
    top, total, dotted = merged(parts[...])
    scale = jnp.exp(own_top[0:1, :] - top) / total
    mean = dotted / total
    mix = (raised[...] * scale) * (slopes[...] - mean)
    mixture[...] = mix.T.astype(BF)
    for parity in range(2):
        pl.when(lax.axis_index("c") != parity)(
            functools.partial(part_product, mixture, w, parity, give)
        )


def keep_kernel(mixture, w, keep):
    for parity in range(2):
        pl.when(lax.axis_index("c") == parity)(
            functools.partial(part_product, mixture, w, parity, keep)
        )


def per_device(hidden, tangent, out_weight):
    rows, width = hidden.shape
    vocab, features = out_weight.shape
    tokens = rows * NZ * NQ
    shape = jax.ShapeDtypeStruct

    with jax.named_scope("gather_z"):
        own = jnp.stack((hidden, tangent))
        block = all_of(jnp.broadcast_to(own[None], (NZ, *own.shape)), "z")
        block = pl.pallas_call(
            turn_kernel,
            out_shape=shape((width, 2 * rows * NZ), BF),
            in_specs=[VMEM],
            out_specs=VMEM,
            compiler_params=pltpu.CompilerParams(vmem_limit_bytes=4 * MIB),
        )(block)
    with jax.named_scope("gather_yx"):
        pieces = {0: block}
        for k in HOPS:
            pieces[k] = send(block, along_yx(k))
        block = jnp.stack([pieces[k] for k in range(NQ)])
        weight = pl.pallas_call(
            load_kernel,
            out_shape=pltpu.VMEM((vocab, features), BF),
            in_specs=[ANY, ANY],
            out_specs=VMEM,
            scratch_shapes=[pltpu.SemaphoreType.DMA],
            cost_estimate=pl.CostEstimate(
                flops=0, transcendentals=0, bytes_accessed=4 * vocab * features
            ),
            compiler_params=pltpu.CompilerParams(vmem_limit_bytes=MIB),
        )(pltpu.with_memory_space_constraint(out_weight, pltpu.HBM), block)
    with jax.named_scope("gather_xy"):
        ahead, behind = send(block, along_xy(3)), send(block, along_xy(1))
        near, far = (send(half, along_xy(2)) for half in (block[: NQ // 2], block[NQ // 2 :]))
        same, weight = lax.optimization_barrier((block, weight))
        own = [near, far, behind, ahead, same]
        theirs = [send(piece, other_core) for piece in own]

    with jax.named_scope("scores"):
        raised, slopes, stats, top = pl.pallas_call(
            scores_kernel,
            out_shape=(
                shape((vocab, tokens), F32),
                shape((vocab, tokens), F32),
                shape((NQ * NQ, 4, tokens), F32),
                shape((4, tokens), F32),
            ),
            in_specs=[VMEM] * 11,
            out_specs=(VMEM,) * 4,
            scratch_shapes=[pltpu.VMEM((features, 2 * tokens), BF)],
            compiler_params=pltpu.CompilerParams(vmem_limit_bytes=20 * MIB),
        )(*own, *theirs, weight)

    with jax.named_scope("statistics"):
        stats = pl.pallas_call(
            merge_kernel,
            out_shape=shape((2 * NZ, 4, tokens), F32),
            in_specs=[VMEM],
            out_specs=VMEM,
            compiler_params=pltpu.CompilerParams(vmem_limit_bytes=4 * MIB),
        )(all_of(stats, ("y", "x")))
        parts = all_of(stats, ("z", "c"))

    with jax.named_scope("product"):
        give, mixture = pl.pallas_call(
            give_kernel,
            out_shape=(
                shape((NQ, NQ, rows * NZ, width), BF),
                shape((tokens, vocab), BF),
            ),
            in_specs=[VMEM] * 5,
            out_specs=(VMEM, VMEM),
            compiler_params=pltpu.CompilerParams(vmem_limit_bytes=8 * MIB),
        )(parts, top, raised, slopes, weight)
        got = send(give, other_core)
        keep = pl.pallas_call(
            keep_kernel,
            out_shape=shape((NQ, NQ, rows * NZ, width), F32),
            in_specs=[VMEM] * 2,
            out_specs=VMEM,
            cost_estimate=pl.CostEstimate(
                flops=vocab * tokens * features,
                transcendentals=0,
                bytes_accessed=2 * vocab * features,
            ),
            compiler_params=pltpu.CompilerParams(vmem_limit_bytes=8 * MIB),
        )(mixture, weight)

    with jax.named_scope("scatter_xy"):
        sums = [keep[k] + got[k].astype(F32) for k in range(NQ)]
        total = sums[0]
        for k in BACK_HOPS:
            total = total + send(sums[k].astype(BF), along_xy(k)).astype(F32)
    with jax.named_scope("scatter_yx"):
        total, rest = total[0], total
        for k in BACK_HOPS:
            total = total + send(rest[k].astype(BF), along_yx(k)).astype(F32)
    with jax.named_scope("scatter_z"):
        total = total.astype(BF).reshape(NZ, rows, width)
        return jnp.sum(all_of(total, "z").astype(F32), axis=0)


def solution(mesh):
    fine = Mesh(mesh.devices.reshape(NZ, NQ, NQ, 2), AXES)
    tokens = P(("z", "y"), ("x", "c"))
    return jax.shard_map(
        per_device,
        mesh=fine,
        in_specs=(tokens, tokens, P(AXES, None)),
        out_specs=tokens,
        check_vma=False,
    )
```

```python
import functools

import jax
import jax.numpy as jnp
from jax import lax
from jax.experimental import pallas as pl
from jax.experimental.pallas import tpu as pltpu
from jax.sharding import Mesh, PartitionSpec as P

AXES = ("z", "y", "x", "c")
BF = jnp.bfloat16
F32 = jnp.float32
VMEM = pl.BlockSpec(memory_space=pltpu.VMEM)
ANY = pl.BlockSpec(memory_space=pl.ANY)
MIB = 1024 * 1024
NZ, NQ = 8, 4


def perm(move):
    pairs = []
    for z in range(NZ):
        for y in range(NQ):
            for x in range(NQ):
                for c in range(2):
                    tz, ty, tx, tc = move(z, y, x, c)
                    src = ((z * NQ + y) * NQ + x) * 2 + c
                    dst = ((tz % NZ * NQ + ty % NQ) * NQ + tx % NQ) * 2 + tc
                    pairs.append((src, dst))
    return pairs


def send(value, move):
    return lax.ppermute(value, AXES, perm(move))


def along_yx(k):
    return lambda z, y, x, c: (z, y + k, x, c) if c == 0 else (z, y, x + k, c)


def along_xy(k):
    return lambda z, y, x, c: (z, y, x + k, c) if c == 0 else (z, y + k, x, c)


def other_core(z, y, x, c):
    return (z, y, x, 1 - c)


HOPS = (1, 3, 2)
BACK_HOPS = (2, 3, 1)


def all_of(value, axes):
    return lax.all_to_all(value, axes, 0, 0)


def turn_kernel(block, out):
    both = block[...].astype(F32)
    rows = [both[:, i].reshape(-1, both.shape[-1]) for i in range(2)]
    out[...] = jnp.concatenate(rows, 0).T.astype(BF)


def load_kernel(w, _, out, sem):
    copy = pltpu.make_async_copy(w, out, sem)
    copy.start()
    copy.wait()


def scores_kernel(*refs):
    own, theirs = refs[:5], refs[5:10]
    w, raised, slopes, stats, tops, whole = refs[10:]
    width, lanes = own[0].shape[1:]
    y, x, c = lax.axis_index("y"), lax.axis_index("x"), lax.axis_index("c")
    for pieces, parity in ((own, c), (theirs, 1 - c)):
        for k in range(NQ):
            for r in range(NQ):
                x_back = jnp.where(parity == 0, k, r)
                y_back = jnp.where(parity == 0, r, k)
                x_at = lax.rem(x + NQ - x_back, NQ)
                y_at = lax.rem(y + NQ - y_back, NQ)
                first = pl.multiple_of((2 * x_at + parity) * width, width)
                column = pl.multiple_of(y_at * lanes, lanes)
                far, near, behind, ahead, same = pieces
                if k == 2:
                    piece = (near, far)[r // 2][r % 2]
                else:
                    piece = (same, behind, None, ahead)[k][r]
                whole[pl.ds(first, width), pl.ds(column, lanes)] = piece

    both = jnp.dot(w[...], whole[...], preferred_element_type=F32)
    low = lax.broadcasted_iota(jnp.int32, (both.shape[0], lanes), 1) < lanes // 2
    for pair in range(NQ // 2):
        first = both[:, 2 * pair * lanes : (2 * pair + 1) * lanes]
        second = both[:, (2 * pair + 1) * lanes : (2 * pair + 2) * lanes]
        columns = slice(pair * lanes, (pair + 1) * lanes)
        raised[:, columns] = jnp.where(low, first, pltpu.roll(second, lanes // 2, 1))
        slopes[:, columns] = jnp.where(low, pltpu.roll(first, lanes // 2, 1), second)

    top = jnp.max(raised[...], axis=0, keepdims=True)
    value = jnp.exp(raised[...] - top)
    raised[...] = value
    total = jnp.sum(value, axis=0, keepdims=True)
    dotted = jnp.sum(value * slopes[...], axis=0, keepdims=True)
    own_stats = jnp.concatenate((top, total, dotted, dotted), 0)
    stats[...] = jnp.broadcast_to(own_stats[None], stats.shape)
    tops[...] = jnp.broadcast_to(top, tops.shape)


def merged(parts):
    tops = parts[:, 0]
    top = jnp.max(tops, axis=0, keepdims=True)
    scale = jnp.exp(tops - top)
    total = jnp.sum(scale * parts[:, 1], axis=0, keepdims=True)
    dotted = jnp.sum(scale * parts[:, 2], axis=0, keepdims=True)
    return top, total, dotted


def merge_kernel(parts, out):
    top, total, dotted = merged(parts[...])
    own = jnp.concatenate((top, total, dotted, dotted), 0)
    out[...] = jnp.broadcast_to(own[None], out.shape)


def part_product(mixture, w, parity, out):
    y, x = lax.axis_index("y"), lax.axis_index("x")
    width, part = out.shape[-1], out.shape[-2]
    for x_of in range(NQ):
        first = (2 * x_of + parity) * width
        start = first // 128 * 128
        stop = -(-(first + width) // 128) * 128
        product = jnp.dot(mixture[...], w[:, start:stop], preferred_element_type=F32)
        piece = product[:, first - start : first - start + width].astype(out.dtype)
        x_ahead = lax.rem(x_of + NQ - x, NQ)
        for y_of in range(NQ):
            y_ahead = lax.rem(y_of + NQ - y, NQ)
            k, r = (x_ahead, y_ahead) if parity == 0 else (y_ahead, x_ahead)
            out[k, r] = piece[y_of * part : (y_of + 1) * part]


def give_kernel(parts, own_top, raised, slopes, w, give, mixture):
    top, total, dotted = merged(parts[...])
    scale = jnp.exp(own_top[0:1, :] - top) / total
    mean = dotted / total
    mix = (raised[...] * scale) * (slopes[...] - mean)
    mixture[...] = mix.T.astype(BF)
    for parity in range(2):
        pl.when(lax.axis_index("c") != parity)(
            functools.partial(part_product, mixture, w, parity, give)
        )


def keep_kernel(mixture, w, keep):
    for parity in range(2):
        pl.when(lax.axis_index("c") == parity)(
            functools.partial(part_product, mixture, w, parity, keep)
        )


def per_device(hidden, tangent, out_weight):
    rows, width = hidden.shape
    vocab, features = out_weight.shape
    tokens = rows * NZ * NQ
    shape = jax.ShapeDtypeStruct

    with jax.named_scope("gather_z"):
        own = jnp.stack((hidden, tangent))
        block = all_of(jnp.broadcast_to(own[None], (NZ, *own.shape)), "z")
        block = pl.pallas_call(
            turn_kernel,
            out_shape=shape((width, 2 * rows * NZ), BF),
            in_specs=[VMEM],
            out_specs=VMEM,
            compiler_params=pltpu.CompilerParams(vmem_limit_bytes=4 * MIB),
        )(block)
    with jax.named_scope("gather_yx"):
        pieces = {0: block}
        for k in HOPS:
            pieces[k] = send(block, along_yx(k))
        block = jnp.stack([pieces[k] for k in range(NQ)])
        weight = pl.pallas_call(
            load_kernel,
            out_shape=pltpu.VMEM((vocab, features), BF),
            in_specs=[ANY, ANY],
            out_specs=VMEM,
            scratch_shapes=[pltpu.SemaphoreType.DMA],
            cost_estimate=pl.CostEstimate(
                flops=0, transcendentals=0, bytes_accessed=4 * vocab * features
            ),
            compiler_params=pltpu.CompilerParams(vmem_limit_bytes=MIB),
        )(pltpu.with_memory_space_constraint(out_weight, pltpu.HBM), block)
    with jax.named_scope("gather_xy"):
        ahead, behind = send(block, along_xy(3)), send(block, along_xy(1))
        near, far = (send(half, along_xy(2)) for half in (block[: NQ // 2], block[NQ // 2 :]))
        same, weight = lax.optimization_barrier((block, weight))
        own = [far, near, behind, ahead, same]
        theirs = [send(piece, other_core) for piece in own]

    with jax.named_scope("scores"):
        raised, slopes, stats, top = pl.pallas_call(
            scores_kernel,
            out_shape=(
                shape((vocab, tokens), F32),
                shape((vocab, tokens), F32),
                shape((NQ * NQ, 4, tokens), F32),
                shape((4, tokens), F32),
            ),
            in_specs=[VMEM] * 11,
            out_specs=(VMEM,) * 4,
            scratch_shapes=[pltpu.VMEM((features, 2 * tokens), BF)],
            compiler_params=pltpu.CompilerParams(vmem_limit_bytes=20 * MIB),
        )(*own, *theirs, weight)

    with jax.named_scope("statistics"):
        stats = pl.pallas_call(
            merge_kernel,
            out_shape=shape((2 * NZ, 4, tokens), F32),
            in_specs=[VMEM],
            out_specs=VMEM,
            compiler_params=pltpu.CompilerParams(vmem_limit_bytes=4 * MIB),
        )(all_of(stats, ("y", "x")))
        parts = all_of(stats, ("z", "c"))

    with jax.named_scope("product"):
        give, mixture = pl.pallas_call(
            give_kernel,
            out_shape=(
                shape((NQ, NQ, rows * NZ, width), BF),
                shape((tokens, vocab), BF),
            ),
            in_specs=[VMEM] * 5,
            out_specs=(VMEM, VMEM),
            compiler_params=pltpu.CompilerParams(vmem_limit_bytes=8 * MIB),
        )(parts, top, raised, slopes, weight)
        got = send(give, other_core)
        keep = pl.pallas_call(
            keep_kernel,
            out_shape=shape((NQ, NQ, rows * NZ, width), F32),
            in_specs=[VMEM] * 2,
            out_specs=VMEM,
            cost_estimate=pl.CostEstimate(
                flops=vocab * tokens * features,
                transcendentals=0,
                bytes_accessed=2 * vocab * features,
            ),
            compiler_params=pltpu.CompilerParams(vmem_limit_bytes=8 * MIB),
        )(mixture, weight)

    with jax.named_scope("scatter_xy"):
        sums = [keep[k] + got[k].astype(F32) for k in range(NQ)]
        total = sums[0]
        for k in BACK_HOPS:
            total = total + send(sums[k].astype(BF), along_xy(k)).astype(F32)
    with jax.named_scope("scatter_yx"):
        total, rest = total[0], total
        for k in BACK_HOPS:
            total = total + send(rest[k].astype(BF), along_yx(k)).astype(F32)
    with jax.named_scope("scatter_z"):
        total = total.astype(BF).reshape(NZ, rows, width)
        return jnp.sum(all_of(total, "z").astype(F32), axis=0)


def solution(mesh):
    fine = Mesh(mesh.devices.reshape(NZ, NQ, NQ, 2), AXES)
    tokens = P(("z", "y"), ("x", "c"))
    return jax.shard_map(
        per_device,
        mesh=fine,
        in_specs=(tokens, tokens, P(AXES, None)),
        out_specs=tokens,
        check_vma=False,
    )
```
